32 devices in a mesh: tm: 32 (over z, y, x, core).
Axes of the slice: x: 2, y: 2, z: 4, core: 2. Of those that a mesh axis runs over, the one named last changes fastest.
Arguments:
- measurements: float32 [32, 128], P('tm'), may hold values from -6 to 6
- noise_levels: float32 [32, 128], P('tm'), may hold values from 0.05 to 2
- transition: float32 [256, 256], replicated, may hold values from -0.5 to 1.5
- sensing: float32 [128, 256], replicated, may hold values from -0.75 to 0.75
- process_noise: float32 [256, 256], replicated, may hold values from -0.2 to 0.6, as said below
- prior_mean: float32 [256], replicated, may hold values from -5 to 5
- prior_covariance: float32 [256, 256], replicated, may hold values from -0.6 to 2.5, as said below
Outputs:
- smoothed_means: float32 [32, 256], P('tm')
- smoothed_covariances: float32 [32, 256, 256], P('tm')
The draws below stay inside these ranges and needn't reach their ends.
Inputs may be any that keep to these rules, and one draw needn't show every extreme that they name: `process_noise`: symmetric positive definite. `prior_covariance`: symmetric positive definite.
All inputs are finite; a program needn't handle non-finite values.
Results may differ from the reference program's by a relative error of at most 0.0003.
Values sent between devices are 32-bit elements; how exact they have to be, the bound alone decides.
No kernel may reach another device: no remote copies, remote signals or barrier semaphores. Data moves between devices by JAX's collectives and lax.ppermute only.
A program may use at most 128 MiB of HBM per device.

```python
import math
import jax
import jax.numpy as jnp
from jax import lax

NS = 256
NO = 128
TIME = 32


def slow_modes(key):
    picks = jax.random.randint(jax.random.fold_in(key, 5), (NS,), 0, 2)
    return picks.astype(jnp.float32)


def definite_matrix(key, scale, floor_low, floor_high):
    first_key, second_key = jax.random.split(key)
    basis = jax.random.truncated_normal(first_key, -4.0, 4.0, (NS, NS), jnp.float32)
    diagonal = jax.random.uniform(second_key, (NS,), jnp.float32, floor_low, floor_high)
    product = jnp.dot(basis, basis.T, precision=lax.Precision.HIGHEST)
    return scale * product / NS + jnp.diag(diagonal)


def draw_transition(key, part):
    slow = slow_modes(key)
    first_key, second_key, third_key = jax.random.split(jax.random.fold_in(key, 7), 3)
    slow_rate = jax.random.uniform(first_key, (NS,), jnp.float32, 0.995, 0.9995)
    fast_rate = jax.random.uniform(second_key, (NS,), jnp.float32, 0.3, 0.6)
    coupling = jax.random.truncated_normal(third_key, -4.0, 4.0, (NS, NS), jnp.float32)
    rates = slow * slow_rate + (1.0 - slow) * fast_rate
    fast_rows = (1.0 - slow)[:, None]
    return jnp.diag(rates) + fast_rows * (0.2 * coupling / jnp.sqrt(jnp.float32(NS)))


def draw_sensing(key, part):
    slow = slow_modes(key)
    values = jax.random.truncated_normal(jax.random.fold_in(key, 13), -4.0, 4.0, (NO, NS), jnp.float32)
    column_scale = slow * 0.05 + (1.0 - slow)
    return values * column_scale[None, :] / jnp.sqrt(jnp.float32(NS))


def draw_process_noise(key, part):
    slow = slow_modes(key)
    mode_scale = slow * 0.1 + (1.0 - slow)
    base = definite_matrix(jax.random.fold_in(key, 11), 0.1, 0.02, 0.2)
    return mode_scale[:, None] * base * mode_scale[None, :]


def draw_prior_covariance(key, part):
    return definite_matrix(jax.random.fold_in(key, 23), 0.5, 0.2, 1.0)


def block_levels(rng, shape, cuts, least, top_value):
    def one(position, shards_of):
        steps = jax.random.uniform(jax.random.fold_in(jax.random.fold_in(rng, 6), position), (shards_of,), jnp.float32, least / len(cuts), top_value / len(cuts))
        return jnp.repeat(jnp.exp(steps), shape[position] // shards_of).reshape((-1,) + (1,) * (len(shape) - position - 1))

    gain = one(*cuts[0])
    for cut in cuts[1:]:
        gain = gain * one(*cut)
    return gain


def bell_draw(stream_key, dims, scale, reach, cuts=(), kind=jnp.bfloat16):
    array = scale * jax.random.normal(stream_key, dims, jnp.float32)
    if cuts:
        array = array * block_levels(stream_key, dims, cuts, -0.22, 0.18)
    return jnp.clip(array, -reach, reach).astype(kind)


def setup_inputs(seed: int = 0) -> dict:
    seeds = jax.random.split(jax.random.key(seed), 8)
    measurements = bell_draw(seeds[0], (TIME, NO), 1.0, 6.0, ((0, 32),), jnp.float32)
    noise_levels = jnp.clip(jnp.exp(math.log(2.0) - 3.6888794 * jax.random.uniform(seeds[1], (TIME, NO), jnp.float32) ** block_levels(seeds[1], (TIME, NO), ((0, 32),), -0.2, 0.2)), 0.05, 2.0)
    transition = draw_transition(jax.random.fold_in(seeds[7], 71), 0)
    sensing = draw_sensing(jax.random.fold_in(seeds[7], 71), 0)
    process_noise = draw_process_noise(jax.random.fold_in(seeds[7], 71), 0)
    prior_mean = bell_draw(seeds[5], (NS,), 1.0, 5.0, (), jnp.float32)
    prior_covariance = draw_prior_covariance(jax.random.fold_in(seeds[7], 71), 0)
    return dict(measurements=measurements, noise_levels=noise_levels, transition=transition, sensing=sensing, process_noise=process_noise, prior_mean=prior_mean, prior_covariance=prior_covariance)


def dense(left, right):
    return jnp.dot(left, right, precision=lax.Precision.HIGHEST)

def lower_solve(factor, values):
    return jax.scipy.linalg.solve_triangular(factor, values, lower=True)

def build_element(measure, levels, sensed, transition, sensing, start_noise, start_center, active):
    state_width = transition.shape[0]
    gain_rows = dense(sensing, start_noise)
    innovation = dense(gain_rows, sensing.T) + jnp.diag(levels)
    factor = jnp.linalg.cholesky(innovation)
    scaled = lower_solve(factor, jnp.concatenate([gain_rows, sensed], axis=1))
    white_gain = scaled[:, :state_width]
    white_sensed = scaled[:, state_width:]
    white_error = lower_solve(factor, measure - dense(sensing, start_center))
    white_measure = lower_solve(factor, measure)
    evolve = active * (transition - dense(white_gain.T, white_sensed))
    offset = start_center + dense(white_gain.T, white_error)
    spread = start_noise - dense(white_gain.T, white_gain)
    info_vector = active * dense(white_sensed.T, white_measure)
    info_matrix = active * dense(white_sensed.T, white_sensed)
    return (evolve, offset, spread, info_vector, info_matrix)

def factors(early_spread, vacancy, late_evolve, late_matrix):
    identity = jnp.eye(early_spread.shape[0], dtype=jnp.float32)
    root_factor = jnp.linalg.cholesky(early_spread + vacancy * identity) * (1.0 - vacancy)
    root_info = dense(root_factor.T, late_matrix)
    inner_factor = jnp.linalg.cholesky(identity + dense(root_info, root_factor))
    carried = lower_solve(inner_factor, dense(root_factor.T, late_evolve.T))
    mixing = lower_solve(inner_factor, root_info)
    return (root_factor, inner_factor, carried, mixing)

def absorb(center, spread, vacancy, element):
    late_evolve, late_offset, late_spread, late_vector, late_matrix = element[:5]
    root_factor, inner_factor, carried, mixing = factors(spread, vacancy, late_evolve, late_matrix)
    through = late_evolve - dense(carried.T, mixing)
    new_center = dense(through, center + dense(spread, late_vector)) + late_offset
    new_spread = dense(carried.T, carried) + late_spread
    return (new_center, new_spread)

def smooth_element(center, spread, transition, process_noise, active):
    forward_map = dense(transition, spread)
    predicted = dense(forward_map, transition.T) + process_noise
    factor = jnp.linalg.cholesky(predicted)
    solved = lower_solve(factor, forward_map)
    back_gain = active * jax.scipy.linalg.solve_triangular(factor, solved, lower=True, trans=1).T
    lift = center - dense(back_gain, dense(transition, center))
    leftover = spread - active * dense(solved.T, solved)
    return (back_gain, lift, leftover)

def reference(measurements, noise_levels, transition, sensing, process_noise, prior_mean, prior_covariance):
    sensed = dense(sensing, transition)
    start_noise = dense(dense(transition, prior_covariance), transition.T) + process_noise
    start_center = dense(transition, prior_mean)
    first_element = build_element(measurements[0], noise_levels[0], sensed, transition, sensing, start_noise, start_center, 0.0)
    zero_center = jnp.zeros_like(prior_mean)
    no_vacancy = jnp.zeros((), jnp.float32)

    def forward(carry, inputs):
        center, spread = carry
        element = build_element(inputs[0], inputs[1], sensed, transition, sensing, process_noise, zero_center, 1.0)
        center, spread = absorb(center, spread, no_vacancy, element)
        return ((center, spread), (center, spread))
    start_state = (first_element[1], first_element[2])
    final_state, filtered_rest = lax.scan(forward, start_state, (measurements[1:], noise_levels[1:]))
    centers = jnp.concatenate([first_element[1][None], filtered_rest[0]], axis=0)
    spreads = jnp.concatenate([first_element[2][None], filtered_rest[1]], axis=0)

    def backward(carry, inputs):
        smooth_center, smooth_spread = carry
        back_gain, lift, leftover = smooth_element(inputs[0], inputs[1], transition, process_noise, 1.0)
        smooth_center = dense(back_gain, smooth_center) + lift
        smooth_spread = dense(dense(back_gain, smooth_spread), back_gain.T) + leftover
        return ((smooth_center, smooth_spread), (smooth_center, smooth_spread))
    last_state = (centers[-1], spreads[-1])
    first_state, smoothed_rest = lax.scan(backward, last_state, (centers[:-1], spreads[:-1]), reverse=True)
    smoothed_means = jnp.concatenate([smoothed_rest[0], centers[-1][None]], axis=0)
    smoothed_covariances = jnp.concatenate([smoothed_rest[1], spreads[-1][None]], axis=0)
    return (smoothed_means, smoothed_covariances)
```

```python
import functools

import jax
import jax.numpy as jnp
from jax import lax
from jax.experimental import pallas as pl
from jax.experimental.pallas import tpu as pltpu
from jax.sharding import PartitionSpec as P

ROWS = 8
LANES = 128


def dot_nn(left, right):
    return lax.dot_general(
        left,
        right,
        (((1,), (0,)), ((), ())),
        precision=lax.Precision.HIGHEST,
        preferred_element_type=jnp.float32,
    )


def dot_nt(left, right):
    return lax.dot_general(
        left,
        right,
        (((1,), (1,)), ((), ())),
        precision=lax.Precision.HIGHEST,
        preferred_element_type=jnp.float32,
    )


def spread_lane(x, lane):
    return jnp.broadcast_to(x[:, lane : lane + 1], x.shape)


def spread_row(x, row):
    return jnp.broadcast_to(x[row : row + 1, :], x.shape)


def recip(x):
    r = pltpu.reciprocal(x, approx=True)
    r = r * (2.0 - x * r)
    return r * (2.0 - x * r)


def factor_small(matrices):
    side = matrices[0].shape[0]
    count = side // ROWS
    shape = (ROWS, side)
    row = lax.broadcasted_iota(jnp.int32, shape, 0)
    lane = lax.broadcasted_iota(jnp.int32, shape, 1)
    panels = [[m[ROWS * k : ROWS * (k + 1)] for k in range(count)] for m in matrices]
    inverses = [
        [jnp.where(lane == row + ROWS * k, 1.0, 0.0) for k in range(count)] for m in matrices
    ]
    outs = [([], []) for m in matrices]
    for k in range(count):
        for A, E, out in zip(panels, inverses, outs):
            cols = [spread_lane(A[k], ROWS * k + i) for i in range(ROWS)]
            pivots = jnp.ones(shape, jnp.float32)
            for i in range(0, ROWS, 2):
                c0, c1 = cols[i], cols[i + 1]
                a = spread_row(c0, i)
                b = spread_row(c0, i + 1)
                c = spread_row(c1, i + 1)
                det = a * c - b * b
                ra = recip(a)
                rdet = recip(det)
                ratio = b * ra
                pivots = jnp.where(row == i, a, pivots)
                pivots = jnp.where(row == i + 1, det * ra, pivots)
                rp = spread_row(A[k], i)
                rq = spread_row(A[k], i + 1) - ratio * rp
                ep = spread_row(E[k], i)
                eq = spread_row(E[k], i + 1) - ratio * ep
                f0 = c0 * ra
                f1 = (a * c1 - b * c0) * rdet
                for q in range(i + 2, ROWS):
                    s0 = spread_row(cols[q], i)
                    s1 = spread_row(cols[q], i + 1) - ratio * s0
                    cols[q] = cols[q] - f0 * s0 - f1 * s1
                m0 = jnp.where(row > i, f0, 0.0)
                m1 = jnp.where(row > i + 1, f1, 0.0)
                A[k] = A[k] - m0 * rp - m1 * rq
                E[k] = E[k] - m0 * ep - m1 * eq
                for j in range(k + 1, count):
                    g0 = spread_lane(A[j], ROWS * k + i)
                    g1 = spread_lane(A[j], ROWS * k + i + 1)
                    h0 = g0 * ra
                    h1 = (a * g1 - b * g0) * rdet
                    A[j] = A[j] - h0 * rp - h1 * rq
                    E[j] = E[j] - h0 * ep - h1 * eq
            s = lax.rsqrt(pivots)
            s = s * (1.5 - 0.5 * pivots * s * s)
            out[0].append(jnp.where(lane >= row + ROWS * k, A[k] * s, 0.0))
            out[1].append(E[k] * s)
    return [(jnp.concatenate(u, axis=0), jnp.concatenate(v, axis=0)) for u, v in outs]


def factor(matrices):
    blocks = matrices[0].shape[0] // LANES
    if blocks == 1:
        return factor_small(matrices)

    def cut(m, i, j):
        return m[LANES * i : LANES * (i + 1), LANES * j : LANES * (j + 1)]

    zero = jnp.zeros((LANES, LANES), jnp.float32)
    uppers = [{} for m in matrices]
    lowers = [{} for m in matrices]
    inverses = [{} for m in matrices]
    for j in range(blocks):
        heads = []
        for m, U, L in zip(matrices, uppers, lowers):
            head = cut(m, j, j)
            for k in range(j):
                head = head - dot_nt(L[j, k], L[j, k])
            heads.append(head)
        for m, U, L, V, (u, v) in zip(matrices, uppers, lowers, inverses, factor_small(heads)):
            U[j, j] = u
            V[j, j] = v
            for i in range(j + 1, blocks):
                right = cut(m, j, i)
                down = cut(m, i, j)
                for k in range(j):
                    right = right - dot_nn(L[j, k], U[k, i])
                    down = down - dot_nn(L[i, k], U[k, j])
                U[j, i] = dot_nn(v, right)
                L[i, j] = dot_nt(down, v)
    outs = []
    for U, L, V in zip(uppers, lowers, inverses):
        for i in range(blocks):
            for j in range(i):
                total = dot_nn(L[i, j], V[j, j])
                for k in range(j + 1, i):
                    total = total + dot_nn(L[i, k], V[k, j])
                V[i, j] = -dot_nn(V[i, i], total)
        whole = [
            jnp.concatenate(
                [
                    jnp.concatenate([D.get((i, j), zero) for j in range(blocks)], axis=1)
                    for i in range(blocks)
                ],
                axis=0,
            )
            for D in (U, V)
        ]
        outs.append(tuple(whole))
    return outs


def unit(side):
    row = lax.broadcasted_iota(jnp.int32, (side, side), 0)
    col = lax.broadcasted_iota(jnp.int32, (side, side), 1)
    return jnp.where(row == col, 1.0, 0.0)


def kernel(
    half,
    place_ref,
    rows_ref,
    transition_ref,
    sensing_ref,
    noise_ref,
    mean_ref,
    prior_ref,
    out_mean_ref,
    out_cov_ref,
    maps,
    consts,
    state,
    info,
):
    n = transition_ref.shape[0]
    o = sensing_ref.shape[0]
    times = rows_ref.shape[0]
    place = place_ref[0]
    late = place >= half
    split = jnp.where(late, place - half, place)

    first_row = lax.broadcasted_iota(jnp.int32, (ROWS, n), 0) == 0
    first_sense = lax.broadcasted_iota(jnp.int32, (ROWS, o), 0) == 0
    eye_sense = unit(o)
    transition = transition_ref[...]
    sensing = sensing_ref[...]
    maps[0:n] = transition
    maps[n:] = dot_nn(sensing, transition)
    noise = noise_ref[...]
    noise_sensed = dot_nt(noise, sensing)
    consts[0:n, 0:n] = noise
    consts[0:n, n:] = noise_sensed
    consts[n:, 0:n] = dot_nn(sensing, noise)
    consts[n:, n:] = dot_nn(sensing, noise_sensed)
    for chain in range(2):
        state[chain, 0:n] = jnp.zeros((n, n), jnp.float32)
        state[chain, n : 2 * n] = unit(n)
        state[chain, 2 * n :] = jnp.zeros((ROWS, n), jnp.float32)
        info[chain] = jnp.zeros((n + ROWS, n), jnp.float32)

    def step(k, carry):
        first = split + 1 - half + k
        first = jnp.where(first < 0, first + times, first)
        second = split + 1 + k

        @pl.when(first == 0)
        def _():
            state[0, 0:n] = prior_ref[...]
            state[0, n : 2 * n] = jnp.zeros((n, n), jnp.float32)
            state[0, 2 * n :] = jnp.where(first_row, mean_ref[...], 0.0)

        ready = []
        for chain, when in ((0, first), (1, second)):
            line = rows_ref[pl.ds(when, 1), :]
            moved = dot_nt(state[chain], maps[...])
            ahead = dot_nn(maps[...], moved[0:n]) + consts[...]
            innovation = ahead[n:, n:] + eye_sense * line[:, o:]
            errors = moved[n:, n:]
            errors = jnp.concatenate(
                [errors[0:n], errors[n:] - jnp.where(first_sense, line[:, 0:o], 0.0)], axis=0
            )
            ready.append((moved, ahead, errors, innovation))
        factors = factor([r[3] for r in ready])
        for chain in range(2):
            moved, ahead, errors, _ = ready[chain]
            white = dot_nt(
                jnp.concatenate([ahead[0:n, n:], errors], axis=0), factors[chain][1]
            )
            before = jnp.concatenate([ahead[0:n, 0:n], moved[n:, 0:n]], axis=0)
            state[chain] = before - dot_nt(white, white[0:n])
            info[chain] = info[chain] + dot_nt(white[n:], white[n : 2 * n])
        return carry

    lax.fori_loop(0, half, step, 0)

    eye = unit(n)
    cut_spread = state[0, 0:n]
    cut_center = state[0, 2 * n :]
    cut_info = info[0, 0:n]
    move = state[1, n : 2 * n]
    mid_spread = state[1, 0:n]
    mid_center = state[1, 2 * n :]
    (mid_root, _), (cut_root, _) = factor([mid_spread, cut_spread])
    rooted = dot_nt(cut_info, mid_root)
    ((_, inner),) = factor([eye + dot_nn(mid_root, rooted)])
    carried = dot_nn(inner, mid_root)
    mixing = dot_nt(rooted, inner)
    kept = cut_info - dot_nt(mixing, mixing)
    early_info = info[1, 0:n] + dot_nt(dot_nn(move, kept), move)
    ((_, last),) = factor([eye + dot_nn(cut_root, dot_nt(early_info, cut_root))])
    residue = -info[0, n:] - dot_nn(mid_center, cut_info)
    residue_carried = dot_nt(residue, carried)
    early_vector = dot_nt(residue - dot_nt(residue_carried, mixing), move) - info[1, n:]
    pull = early_vector - dot_nn(cut_center, early_info)
    cut_root_t = cut_root.T
    through = move - dot_nn(dot_nn(move, mixing), carried)
    through_center = mid_center + dot_nn(residue_carried, carried)
    carried_t = carried.T
    leftover = dot_nt(carried_t, carried_t)
    late_root = dot_nt(through.T, cut_root)
    early_root = dot_nt(cut_root_t, last)
    early_center = cut_center + dot_nt(dot_nn(pull, early_root), early_root)
    root = dot_nt(jnp.where(late, late_root, cut_root_t), last)
    out_cov_ref[0] = jnp.where(late, leftover, 0.0) + dot_nt(root, root)
    late_center = dot_nn(early_center, through) + through_center
    out_mean_ref[...] = jnp.where(late, late_center, early_center)[0:1]


def shards(
    measurements, noise_levels, transition, sensing, process_noise, prior_mean, prior_covariance
):
    state_width = transition.shape[0]
    sense_width = sensing.shape[0]
    devices = lax.axis_size("tm")
    half = devices // 2
    place = lax.axis_index("tm").astype(jnp.int32).reshape(1)
    rows = jnp.concatenate([measurements, noise_levels], axis=1)
    rows = lax.all_gather(rows, "tm", axis=0, tiled=True)
    tall = state_width + sense_width
    vmem = pl.BlockSpec(memory_space=pltpu.VMEM)
    return pl.pallas_call(
        functools.partial(kernel, half),
        out_shape=(
            jax.ShapeDtypeStruct((1, state_width), jnp.float32),
            jax.ShapeDtypeStruct((1, state_width, state_width), jnp.float32),
        ),
        in_specs=[pl.BlockSpec(memory_space=pltpu.SMEM)] + [vmem] * 6,
        out_specs=(vmem, vmem),
        scratch_shapes=[
            pltpu.VMEM((tall, state_width), jnp.float32),
            pltpu.VMEM((tall, tall), jnp.float32),
            pltpu.VMEM((2, 2 * state_width + ROWS, state_width), jnp.float32),
            pltpu.VMEM((2, state_width + ROWS, state_width), jnp.float32),
        ],
        compiler_params=pltpu.CompilerParams(vmem_limit_bytes=48 * 1024 * 1024),
    )(
        place,
        rows,
        transition,
        sensing,
        process_noise,
        prior_mean.reshape(1, state_width),
        prior_covariance,
    )


def solution(mesh):
    return jax.shard_map(
        shards,
        mesh=mesh,
        in_specs=(P("tm", None), P("tm", None), P(), P(), P(), P(), P()),
        out_specs=(P("tm", None), P("tm", None, None)),
        check_vma=False,
    )
```

```python
import functools

import jax
import jax.numpy as jnp
from jax import lax
from jax.experimental import pallas as pl
from jax.experimental.pallas import tpu as pltpu
from jax.sharding import PartitionSpec as P

ROWS = 8
LANES = 128
GROUP = 4
BOARD = ROWS * ROWS + ROWS * ROWS // 2
FAN = 4


def dot_nn(left, right):
    return lax.dot_general(
        left,
        right,
        (((1,), (0,)), ((), ())),
        precision=lax.Precision.HIGHEST,
        preferred_element_type=jnp.float32,
    )


def dot_nt(left, right):
    return lax.dot_general(
        left,
        right,
        (((1,), (1,)), ((), ())),
        precision=lax.Precision.HIGHEST,
        preferred_element_type=jnp.float32,
    )


def spread_lane(x, lane):
    return jnp.broadcast_to(x[:, lane : lane + 1], x.shape)


def dot_tn(left, right):
    return lax.dot_general(
        left,
        right,
        (((0,), (0,)), ((), ())),
        precision=lax.Precision.HIGHEST,
        preferred_element_type=jnp.float32,
    )


def factor_small(matrices, board, group):
    side = matrices[0].shape[0]
    count = side // ROWS
    group = min(group, count)
    shape = (ROWS, side)
    row = lax.broadcasted_iota(jnp.int32, shape, 0)
    lane = lax.broadcasted_iota(jnp.int32, shape, 1)
    tasks = [[m[ROWS * k : ROWS * (k + 1)] for k in range(count)] for m in matrices]
    outs = [([], []) for m in matrices]
    for k in range(count):
        base = ROWS * k
        stop = min(count, (k // group + 1) * group)
        for t, (X, out) in enumerate(zip(tasks, outs)):

            def put(slot, values):
                board[t, k % 2, ROWS * slot : ROWS * (slot + 1)] = values

            def spread(slot, r):
                at = ROWS * slot + r
                return jnp.broadcast_to(board[t, k % 2, at : at + 1], shape)

            cols = [spread_lane(X[k], base + i) for i in range(ROWS)]
            for i in range(ROWS):
                put(i, cols[i])
            block = {(r, i): spread(i, r) for i in range(ROWS) for r in range(i, ROWS)}
            nexts = [spread_lane(X[k + 1], base + i) for i in range(ROWS)] if k + 1 < stop else []
            pivots = jnp.ones(shape, jnp.float32)
            for i in range(0, ROWS, 2):
                p = base + i
                pair = (lane == p) | (lane == p + 1)
                a, b, c = block[i, i], block[i + 1, i], block[i + 1, i + 1]
                det = a * c - b * b
                ra = pltpu.reciprocal(a, approx=True)
                rdet = pltpu.reciprocal(det, approx=True)
                ratio = b * ra
                rest = range(i + 2, ROWS)
                firsts = {q: block[q, i] for q in rest}
                mixed = {q: a * block[q, i + 1] - b * firsts[q] for q in rest}
                seconds = {q: mixed[q] * ra for q in rest}
                for q in rest:
                    for r in range(q, ROWS):
                        block[r, q] = (
                            block[r, q] - (firsts[r] * ra) * firsts[q] - (mixed[r] * rdet) * seconds[q]
                        )
                pivots = jnp.where(row == i, a, pivots)
                pivots = jnp.where(row == i + 1, det * ra, pivots)
                put(ROWS + i // 2, X[k])
                xp = spread(ROWS + i // 2, i)
                xp = jnp.where(lane == p, 1.0, jnp.where(lane == p + 1, 0.0, xp))
                xq = spread(ROWS + i // 2, i + 1)
                xq = jnp.where(lane == p + 1, 1.0, jnp.where(lane == p, 0.0, xq))
                xq = xq - ratio * xp
                Z = jnp.where((row == i) & (lane == p), 1.0, X[k])
                if i + 2 < ROWS:
                    f0 = cols[i] * ra
                    f1 = (a * cols[i + 1] - b * cols[i]) * rdet
                    for q in rest:
                        cols[q] = cols[q] - f0 * firsts[q] - f1 * seconds[q]
                    m0 = jnp.where(row > i + 1, f0, 0.0)
                    m1 = jnp.where(row > i + 1, f1, 0.0)
                    Z = jnp.where((row > i + 1) & pair, 0.0, Z) - m0 * xp - m1 * xq
                X[k] = jnp.where(row == i + 1, xq, Z)
                for j in range(k + 1, stop):
                    if j == k + 1:
                        g0, g1 = nexts[i], nexts[i + 1]
                    else:
                        g0 = spread_lane(X[j], p)
                        g1 = spread_lane(X[j], p + 1)
                    h0 = g0 * ra
                    h1 = (a * g1 - b * g0) * rdet
                    if j == k + 1:
                        for q in rest:
                            nexts[q] = nexts[q] - h0 * firsts[q] - h1 * seconds[q]
                    X[j] = jnp.where(pair, 0.0, X[j]) - h0 * xp - h1 * xq
            s = lax.rsqrt(pivots)
            s = s * (1.5 - 0.5 * pivots * s * s)
            scaled = X[k] * s
            diagonal = jnp.where(lane == row + base, pivots * s, 0.0)
            out[0].append(jnp.where(lane > row + base, scaled, diagonal))
            out[1].append(jnp.where(lane <= row + base, scaled, 0.0))
        if k + 1 == stop and stop < count:
            begin = stop - group
            low, high = ROWS * begin, ROWS * stop
            for X, out in zip(tasks, outs):
                uppers = jnp.concatenate(out[0][begin:stop], axis=0)
                lowers = jnp.concatenate(out[1][begin:stop], axis=0)
                after = lax.broadcasted_iota(jnp.int32, uppers.shape, 1) >= high
                change = dot_tn(uppers, jnp.where(after, uppers, lowers))
                here = (lane >= low) & (lane < high)
                for j in range(stop, count):
                    X[j] = jnp.where(here, 0.0, X[j]) - change[ROWS * j : ROWS * (j + 1)]
    return [(jnp.concatenate(u, axis=0), jnp.concatenate(v, axis=0)) for u, v in outs]


def factor(matrices, board):
    blocks = matrices[0].shape[0] // LANES
    if blocks == 1:
        return factor_small(matrices, board, GROUP)

    def cut(m, i, j):
        return m[LANES * i : LANES * (i + 1), LANES * j : LANES * (j + 1)]

    zero = jnp.zeros((LANES, LANES), jnp.float32)
    uppers = [{} for m in matrices]
    lowers = [{} for m in matrices]
    inverses = [{} for m in matrices]
    for j in range(blocks):
        heads = []
        for m, U, L in zip(matrices, uppers, lowers):
            head = cut(m, j, j)
            for k in range(j):
                head = head - dot_nt(L[j, k], L[j, k])
            heads.append(head)
        for m, U, L, V, (u, v) in zip(
            matrices, uppers, lowers, inverses, factor_small(heads, board, GROUP)
        ):
            U[j, j] = u
            V[j, j] = v
            for i in range(j + 1, blocks):
                right = cut(m, j, i)
                down = cut(m, i, j)
                for k in range(j):
                    right = right - dot_nn(L[j, k], U[k, i])
                    down = down - dot_nn(L[i, k], U[k, j])
                U[j, i] = dot_nn(v, right)
                L[i, j] = dot_nt(down, v)
    outs = []
    for U, L, V in zip(uppers, lowers, inverses):
        for i in range(blocks):
            for j in range(i):
                total = dot_nn(L[i, j], V[j, j])
                for k in range(j + 1, i):
                    total = total + dot_nn(L[i, k], V[k, j])
                V[i, j] = -dot_nn(V[i, i], total)
        whole = [
            jnp.concatenate(
                [
                    jnp.concatenate([D.get((i, j), zero) for j in range(blocks)], axis=1)
                    for i in range(blocks)
                ],
                axis=0,
            )
            for D in (U, V)
        ]
        outs.append(tuple(whole))
    return outs


def unit(side):
    row = lax.broadcasted_iota(jnp.int32, (side, side), 0)
    col = lax.broadcasted_iota(jnp.int32, (side, side), 1)
    return jnp.where(row == col, 1.0, 0.0)


def first_of(values):
    row = lax.broadcasted_iota(jnp.int32, (ROWS, values.shape[1]), 0)
    return jnp.where(row == 0, values, 0.0)


def maps_kernel(transition_ref, sensing_ref, noise_ref, maps_ref, consts_ref):
    n = transition_ref.shape[0]
    transition = transition_ref[...]
    sensing = sensing_ref[...]
    noise = noise_ref[...]
    maps_ref[0:n] = transition
    maps_ref[n:] = dot_nn(sensing, transition)
    noise_sensed = dot_nt(noise, sensing)
    consts_ref[0:n, 0:n] = noise
    consts_ref[0:n, n:] = noise_sensed
    consts_ref[n:, 0:n] = jnp.zeros((sensing.shape[0], n), jnp.float32)
    consts_ref[n:, n:] = dot_nn(sensing, noise_sensed)


def window_kernel(
    steps,
    times,
    begin_ref,
    rows_ref,
    maps_ref,
    consts_ref,
    mean_ref,
    prior_ref,
    state_ref,
    info_ref,
    moved_ref,
    waiting_ref,
    inverse_ref,
    sensed_ref,
    board,
):
    n = prior_ref.shape[0]
    o = maps_ref.shape[0] - n
    begin = begin_ref[0]
    eye_sense = unit(o)

    def wrap(t):
        return jnp.where(t >= times, t - times, t)

    def line_at(k):
        return rows_ref[pl.ds(jnp.minimum(k, steps - 1), 1), :]

    def first_spread(k, spread):
        line = line_at(k)
        return spread + consts_ref[n:, n:] + eye_sense * line[:, o:]

    moved_ref[0:n] = jnp.zeros((n, n), jnp.float32)
    moved_ref[n : 2 * n] = unit(n)
    moved_ref[2 * n :] = jnp.zeros((ROWS, n), jnp.float32)
    waiting_ref[...] = jnp.zeros_like(waiting_ref)
    inverse_ref[...] = jnp.zeros_like(inverse_ref)
    info_ref[...] = jnp.zeros_like(info_ref)
    sensed = maps_ref[n:]
    fresh = begin == 0
    sensed_ref[...] = first_spread(
        0, jnp.where(fresh, dot_nn(sensed, dot_nt(prior_ref[...], sensed)), 0.0)
    )

    def update():
        white = dot_nt(waiting_ref[...], inverse_ref[...])
        info_ref[...] = info_ref[...] + dot_nt(white[n:], white[n : 2 * n])
        return moved_ref[...] - dot_nt(white, white[0:n])

    def step(k, carry):
        ((_, inverse),) = factor_small([sensed_ref[...]], board, o // ROWS)
        now = wrap(begin + k)
        later = wrap(now + 1)
        state = update()
        state = jnp.where(
            now == 0,
            jnp.concatenate(
                [prior_ref[...], jnp.zeros((n, n), jnp.float32), first_of(mean_ref[...])], axis=0
            ),
            state,
        )
        moved = dot_nt(state, maps_ref[...])
        ahead = dot_nn(maps_ref[0:n], moved[0:n]) + consts_ref[0:n]
        moved_ref[0:n] = ahead[:, 0:n]
        moved_ref[n:] = moved[n:, 0:n]
        waiting_ref[0:n] = ahead[:, n:]
        waiting_ref[n : 2 * n] = moved[n : 2 * n, n:]
        waiting_ref[2 * n :] = moved[2 * n :, n:] - first_of(line_at(k)[:, 0:o])
        spread = jnp.where(later == 0, prior_ref[...], ahead[:, 0:n])
        kept = dot_nn(maps_ref[n:], dot_nt(spread, maps_ref[n:]))
        gained = dot_nt(dot_nn(maps_ref[n:], ahead[:, n:]), inverse)
        gained = jnp.where(later == 0, 0.0, gained)
        sensed_ref[...] = first_spread(k + 1, kept - dot_nt(gained, gained))
        inverse_ref[...] = inverse
        return carry

    lax.fori_loop(0, steps, step, 0)
    state_ref[...] = update()


def meet_kernel(
    role_ref, state_ref, info_ref, far_state_ref, far_info_ref, mean_ref, cov_ref, board
):
    n = state_ref.shape[1]
    late = role_ref[0] == 1
    eye = unit(n)

    def of_cut(rows, near, far):
        return jnp.where(late, far[rows], near[rows])

    def of_middle(rows, near, far):
        return jnp.where(late, near[rows], far[rows])

    spread_rows, move_rows, center_rows = slice(0, n), slice(n, 2 * n), slice(2 * n, 2 * n + ROWS)
    info_rows, vector_rows = slice(0, n), slice(n, n + ROWS)
    cut_spread = of_cut(spread_rows, state_ref, far_state_ref)
    cut_center = of_cut(center_rows, state_ref, far_state_ref)
    cut_info = of_cut(info_rows, info_ref, far_info_ref)
    cut_vector = of_cut(vector_rows, info_ref, far_info_ref)
    mid_spread = of_middle(spread_rows, state_ref, far_state_ref)
    move = of_middle(move_rows, state_ref, far_state_ref)
    mid_center = of_middle(center_rows, state_ref, far_state_ref)
    mid_info = of_middle(info_rows, info_ref, far_info_ref)
    mid_vector = of_middle(vector_rows, info_ref, far_info_ref)

    (mid_root, _), (cut_root, _) = factor([mid_spread, cut_spread], board)
    rooted = dot_nt(cut_info, mid_root)
    ((_, inner),) = factor([eye + dot_nn(mid_root, rooted)], board)
    carried = dot_nn(inner, mid_root)
    mixing = dot_nt(rooted, inner)
    kept = cut_info - dot_nt(mixing, mixing)
    early_info = mid_info + dot_nt(dot_nn(move, kept), move)
    ((_, last),) = factor(
        [eye + dot_nn(cut_root, dot_nt(early_info, cut_root))], board
    )
    residue = -cut_vector - dot_nn(mid_center, cut_info)
    residue_carried = dot_nt(residue, carried)
    early_vector = dot_nt(residue - dot_nt(residue_carried, mixing), move) - mid_vector
    pull = early_vector - dot_nn(cut_center, early_info)
    cut_root_t = cut_root.T
    through = move - dot_nn(dot_nn(move, mixing), carried)
    through_center = mid_center + dot_nn(residue_carried, carried)
    carried_t = carried.T
    leftover = dot_nt(carried_t, carried_t)
    late_root = dot_nt(through.T, cut_root)
    early_root = dot_nt(cut_root_t, last)
    early_center = cut_center + dot_nt(dot_nn(pull, early_root), early_root)
    root = dot_nt(jnp.where(late, late_root, cut_root_t), last)
    cov_ref[0] = jnp.where(late, leftover, 0.0) + dot_nt(root, root)
    late_center = dot_nn(early_center, through) + through_center
    mean_ref[...] = jnp.where(late, late_center, early_center)[0:1]


def begin_of(device, devices):
    quarter = devices // 4
    chip = device // 2
    upper = chip // quarter
    split = 2 * (chip - quarter * upper) + upper
    role = device % 2
    return (split + 1 + (1 - role) * (devices - devices // 2)) % devices


def gather_rows(rows, steps, axis):
    devices = lax.axis_size(axis)
    begins = [begin_of(i, devices) for i in range(devices)]
    holder = {begin: i for i, begin in enumerate(begins)}
    held = min(FAN, steps)
    parts = [
        lax.ppermute(rows, axis, [((begins[i] + j) % devices, i) for i in range(devices)])
        for j in range(held)
    ]
    rows = jnp.concatenate(parts, axis=0)
    while held < steps:
        parts = [rows]
        for m in range(1, FAN):
            size = min(held, steps - m * held)
            if size > 0:
                pairs = [(holder[(begins[i] + m * held) % devices], i) for i in range(devices)]
                parts.append(lax.ppermute(rows[:size], axis, pairs))
        rows = jnp.concatenate(parts, axis=0)
        held = min(steps, FAN * held)
    return rows


def shards(
    measurements, noise_levels, transition, sensing, process_noise, prior_mean, prior_covariance
):
    n = transition.shape[0]
    o = sensing.shape[0]
    devices = lax.axis_size("tm")
    half = devices // 2
    device = lax.axis_index("tm").astype(jnp.int32)
    role = device % 2
    begin = begin_of(device, devices)

    rows = gather_rows(jnp.concatenate([measurements, noise_levels], axis=1), half, "tm")
    vmem = pl.BlockSpec(memory_space=pltpu.VMEM)
    smem = pl.BlockSpec(memory_space=pltpu.SMEM)
    params = pltpu.CompilerParams(vmem_limit_bytes=48 * 1024 * 1024)

    def shape(*dims):
        return jax.ShapeDtypeStruct(dims, jnp.float32)

    maps, consts = pl.pallas_call(
        maps_kernel,
        out_shape=(shape(n + o, n), shape(n + o, n + o)),
        in_specs=[vmem] * 3,
        out_specs=(vmem, vmem),
        compiler_params=params,
    )(transition, sensing, process_noise)
    state, info = pl.pallas_call(
        functools.partial(window_kernel, half, devices),
        out_shape=(shape(2 * n + ROWS, n), shape(n + ROWS, n)),
        in_specs=[smem] + [vmem] * 5,
        out_specs=(vmem, vmem),
        scratch_shapes=[
            pltpu.VMEM((2 * n + ROWS, n), jnp.float32),
            pltpu.VMEM((2 * n + ROWS, o), jnp.float32),
            pltpu.VMEM((o, o), jnp.float32),
            pltpu.VMEM((o, o), jnp.float32),
            pltpu.VMEM((1, 2, BOARD, o), jnp.float32),
        ],
        compiler_params=params,
    )(begin.reshape(1), rows, maps, consts, prior_mean.reshape(1, n), prior_covariance)
    swap = [(i, i ^ 1) for i in range(devices)]
    far_state = lax.ppermute(state, "tm", swap)
    far_info = lax.ppermute(info, "tm", swap)
    mean, cov = pl.pallas_call(
        meet_kernel,
        out_shape=(shape(1, n), shape(1, n, n)),
        in_specs=[smem] + [vmem] * 4,
        out_specs=(vmem, vmem),
        scratch_shapes=[pltpu.VMEM((2, 2, BOARD, LANES), jnp.float32)],
        compiler_params=params,
    )(role.reshape(1), state, info, far_state, far_info)
    home = []
    for i in range(devices):
        above = i >= half
        spot = 2 * ((i - half if above else i) // 2) + (1 if above else 0)
        home.append((i, spot + half if i % 2 else spot))
    return lax.ppermute(mean, "tm", home), lax.ppermute(cov, "tm", home)


def solution(mesh):
    return jax.shard_map(
        shards,
        mesh=mesh,
        in_specs=(P("tm", None), P("tm", None), P(), P(), P(), P(), P()),
        out_specs=(P("tm", None), P("tm", None, None)),
        check_vma=False,
    )
```

```python
import functools

import jax
import jax.numpy as jnp
from jax import lax
from jax.experimental import pallas as pl
from jax.experimental.pallas import tpu as pltpu
from jax.sharding import PartitionSpec as P

ROWS = 8
LANES = 128
GROUP = 4
LEAD = 1
VECTOR = 16
EXTRA = ROWS + ROWS // 2
BOARD = ROWS * (EXTRA + ROWS)
FAN = 4


def dot_nn(left, right):
    return lax.dot_general(
        left,
        right,
        (((1,), (0,)), ((), ())),
        precision=lax.Precision.HIGHEST,
        preferred_element_type=jnp.float32,
    )


def dot_nt(left, right):
    return lax.dot_general(
        left,
        right,
        (((1,), (1,)), ((), ())),
        precision=lax.Precision.HIGHEST,
        preferred_element_type=jnp.float32,
    )


def pieces(x, count):
    out = []
    for _ in range(count):
        out.append(x.astype(jnp.bfloat16))
        x = x - out[-1].astype(jnp.float32)
    return out


def left_of(x):
    high, low = pieces(x, 2)
    return jnp.concatenate([high, low, high], axis=1)


def right_of(x):
    high, low = pieces(x, 2)
    return jnp.concatenate([high, high, low], axis=1)


def left_moving(x):
    high, low = pieces(x, 2)
    return jnp.concatenate([high, low, high, high], axis=1)


def right_moving(x):
    high, low = pieces(x, 2)
    return jnp.concatenate([high, high, high, low], axis=0)


def join_nn(left, right):
    return lax.dot_general(
        left, right, (((1,), (0,)), ((), ())), preferred_element_type=jnp.float32
    )


def join_nt(left, right):
    return lax.dot_general(
        left, right, (((1,), (1,)), ((), ())), preferred_element_type=jnp.float32
    )


def spread_lane(x, lane):
    return jnp.broadcast_to(x[:, lane : lane + 1], x.shape)


def exact_tn(left, right):
    a, b, c = pieces(left, 3)
    p, q, r = pieces(right, 3)
    return lax.dot_general(
        jnp.concatenate([a, a, b, a, b, c], axis=0),
        jnp.concatenate([p, q, p, r, q, p], axis=0),
        (((0,), (0,)), ((), ())),
        preferred_element_type=jnp.float32,
    )


def exact_nt(left, right):
    a, b, c = pieces(left, 3)
    p, q, r = pieces(right, 3)
    return join_nt(
        jnp.concatenate([a, a, b, a, b, c], axis=1), jnp.concatenate([p, q, p, r, q, p], axis=1)
    )


def exact_nn(left, right):
    a, b, c = pieces(left, 3)
    p, q, r = pieces(right, 3)
    return join_nn(
        jnp.concatenate([a, a, b, a, b, c], axis=1), jnp.concatenate([p, q, p, r, q, p], axis=0)
    )


def near_nn(left, right):
    high, low = pieces(right, 2)
    return join_nn(left_of(left), jnp.concatenate([high, high, low], axis=0))


def near_nt(left, right):
    return join_nt(left_of(left), right_of(right))


def factor_small(matrices, board, group):
    side = matrices[0].shape[0]
    count = side // ROWS
    group = min(group, count)
    shape = (ROWS, side)
    row = lax.broadcasted_iota(jnp.int32, shape, 0)
    lane = lax.broadcasted_iota(jnp.int32, shape, 1)
    tasks = [[m[ROWS * k : ROWS * (k + 1)] for k in range(count)] for m in matrices]
    outs = [([], []) for m in matrices]
    heads = [[spread_lane(X[0], i) for i in range(ROWS)] for X in tasks]
    for k in range(count):
        base = ROWS * k
        more = k + 1 < count
        stop = min(count, (k // group + 1) * group)
        reach = min(count, stop + LEAD)
        for t, (X, out) in enumerate(zip(tasks, outs)):

            def put(slot, values):
                board[t, k % 2, ROWS * slot : ROWS * (slot + 1)] = values

            def spread(slot, r):
                at = ROWS * slot + r
                return jnp.broadcast_to(board[t, k % 2, at : at + 1], shape)

            cols = heads[t]
            for i in range(ROWS):
                put(i, cols[i])
            block = {(r, i): spread(i, r) for i in range(ROWS) for r in range(i, ROWS)}
            nexts = [spread_lane(X[k + 1], base + i) for i in range(ROWS)] if more else []
            heads[t] = [spread_lane(X[k + 1], base + ROWS + i) for i in range(ROWS)] if more else []
            pivots = jnp.ones(shape, jnp.float32)
            for i in range(0, ROWS, 2):
                p = base + i
                pair = (lane == p) | (lane == p + 1)
                a, b, c = block[i, i], block[i + 1, i], block[i + 1, i + 1]
                det = a * c - b * b
                ra = pltpu.reciprocal(a, approx=True)
                rdet = pltpu.reciprocal(det, approx=True)
                ratio = b * ra
                rest = range(i + 2, ROWS)
                firsts = {q: block[q, i] for q in rest}
                mixed = {q: a * block[q, i + 1] - b * firsts[q] for q in rest}
                seconds = {q: mixed[q] * ra for q in rest}
                for q in rest:
                    for r in range(q, ROWS):
                        block[r, q] = (
                            block[r, q] - (firsts[r] * ra) * firsts[q] - (mixed[r] * rdet) * seconds[q]
                        )
                pivots = jnp.where(row == i, a, pivots)
                pivots = jnp.where(row == i + 1, det * ra, pivots)
                put(ROWS + i // 2, X[k])
                xp = spread(ROWS + i // 2, i)
                xp = jnp.where(lane == p, 1.0, jnp.where(lane == p + 1, 0.0, xp))
                xq = spread(ROWS + i // 2, i + 1)
                xq = jnp.where(lane == p + 1, 1.0, jnp.where(lane == p, 0.0, xq))
                xq = xq - ratio * xp
                Z = jnp.where((row == i) & (lane == p), 1.0, X[k])
                if i + 2 < ROWS:
                    f0 = cols[i] * ra
                    f1 = (a * cols[i + 1] - b * cols[i]) * rdet
                    for q in rest:
                        cols[q] = cols[q] - f0 * firsts[q] - f1 * seconds[q]
                    m0 = jnp.where(row > i + 1, f0, 0.0)
                    m1 = jnp.where(row > i + 1, f1, 0.0)
                    Z = jnp.where((row > i + 1) & pair, 0.0, Z) - m0 * xp - m1 * xq
                X[k] = jnp.where(row == i + 1, xq, Z)
                for j in range(k + 1, reach):
                    if j == k + 1:
                        g0, g1 = nexts[i], nexts[i + 1]
                    else:
                        g0 = spread_lane(X[j], p)
                        g1 = spread_lane(X[j], p + 1)
                    h0 = g0 * ra
                    g1 = a * g1 - b * g0
                    h1 = g1 * rdet
                    if j == k + 1:
                        put(EXTRA + i, g0)
                        put(EXTRA + i + 1, g1 * ra)
                        for q in range(ROWS):
                            first, second = spread(EXTRA + i, q), spread(EXTRA + i + 1, q)
                            heads[t][q] = heads[t][q] - h0 * first - h1 * second
                        for q in rest:
                            nexts[q] = nexts[q] - h0 * firsts[q] - h1 * seconds[q]
                    X[j] = jnp.where(pair, 0.0, X[j]) - h0 * xp - h1 * xq
            s = lax.rsqrt(pivots)
            s = s * (1.5 - 0.5 * pivots * s * s)
            scaled = X[k] * s
            diagonal = jnp.where(lane == row + base, pivots * s, 0.0)
            out[0].append(jnp.where(lane > row + base, scaled, diagonal))
            out[1].append(jnp.where(lane <= row + base, scaled, 0.0))
        if k + 1 == stop and reach < count:
            begin = stop - group
            low, high = ROWS * begin, ROWS * stop
            for X, out in zip(tasks, outs):
                uppers = jnp.concatenate(out[0][begin:stop], axis=0)
                lowers = jnp.concatenate(out[1][begin:stop], axis=0)
                after = lax.broadcasted_iota(jnp.int32, uppers.shape, 1) >= high
                change = exact_tn(uppers, jnp.where(after, uppers, lowers))
                here = (lane >= low) & (lane < high)
                for j in range(reach, count):
                    X[j] = jnp.where(here, 0.0, X[j]) - change[ROWS * j : ROWS * (j + 1)]
    return [(jnp.concatenate(u, axis=0), jnp.concatenate(v, axis=0)) for u, v in outs]


def factor(matrices, board):
    blocks = matrices[0].shape[0] // LANES
    if blocks == 1:
        return factor_small(matrices, board, GROUP)

    def cut(m, i, j):
        return m[LANES * i : LANES * (i + 1), LANES * j : LANES * (j + 1)]

    zero = jnp.zeros((LANES, LANES), jnp.float32)
    uppers = [{} for m in matrices]
    lowers = [{} for m in matrices]
    inverses = [{} for m in matrices]
    for j in range(blocks):
        heads = []
        for m, U, L in zip(matrices, uppers, lowers):
            head = cut(m, j, j)
            for k in range(j):
                head = head - exact_nt(L[j, k], L[j, k])
            heads.append(head)
        for m, U, L, V, (u, v) in zip(
            matrices, uppers, lowers, inverses, factor_small(heads, board, GROUP)
        ):
            U[j, j] = u
            V[j, j] = v
            for i in range(j + 1, blocks):
                right = cut(m, j, i)
                down = cut(m, i, j)
                for k in range(j):
                    right = right - exact_nn(L[j, k], U[k, i])
                    down = down - exact_nn(L[i, k], U[k, j])
                U[j, i] = exact_nn(v, right)
                L[i, j] = exact_nt(down, v)
    outs = []
    for U, L, V in zip(uppers, lowers, inverses):
        for i in range(blocks):
            for j in range(i):
                total = exact_nn(L[i, j], V[j, j])
                for k in range(j + 1, i):
                    total = total + exact_nn(L[i, k], V[k, j])
                V[i, j] = -exact_nn(V[i, i], total)
        whole = [
            jnp.concatenate(
                [
                    jnp.concatenate([D.get((i, j), zero) for j in range(blocks)], axis=1)
                    for i in range(blocks)
                ],
                axis=0,
            )
            for D in (U, V)
        ]
        outs.append(tuple(whole))
    return outs


def unit(side):
    row = lax.broadcasted_iota(jnp.int32, (side, side), 0)
    col = lax.broadcasted_iota(jnp.int32, (side, side), 1)
    return jnp.where(row == col, 1.0, 0.0)


def first_of(values):
    row = lax.broadcasted_iota(jnp.int32, (VECTOR, values.shape[1]), 0)
    return jnp.where(row == 0, values, 0.0)


def maps_kernel(transition_ref, sensing_ref, noise_ref, left_ref, right_ref, consts_ref):
    n = transition_ref.shape[0]
    transition = transition_ref[...]
    sensing = sensing_ref[...]
    noise = noise_ref[...]
    maps = jnp.concatenate([transition, dot_nn(sensing, transition)], axis=0)
    high, low, least = pieces(maps, 3)
    left_ref[...] = jnp.concatenate([high, low, least, high], axis=1)
    right_ref[...] = jnp.concatenate([high, high, low, least], axis=1)
    noise_sensed = dot_nt(noise, sensing)
    consts_ref[0:n, 0:n] = noise
    consts_ref[0:n, n:] = noise_sensed
    consts_ref[n:, 0:n] = jnp.zeros((sensing.shape[0], n), jnp.float32)
    consts_ref[n:, n:] = dot_nn(sensing, noise_sensed)


def window_kernel(
    steps,
    times,
    begin_ref,
    rows_ref,
    left_ref,
    right_ref,
    consts_ref,
    mean_ref,
    prior_ref,
    state_ref,
    info_ref,
    moved_ref,
    waiting_ref,
    inverse_ref,
    sensed_ref,
    board,
):
    n = prior_ref.shape[0]
    o = left_ref.shape[0] - n
    begin = begin_ref[0]
    eye_sense = unit(o)

    def wrap(t):
        return jnp.where(t >= times, t - times, t)

    def line_at(k):
        return rows_ref[pl.ds(jnp.minimum(k, steps - 1), 1), :]

    def first_spread(k, spread):
        line = line_at(k)
        return spread + consts_ref[n:, n:] + eye_sense * line[:, o:]

    moved_ref[0:n] = jnp.zeros((n, n), jnp.float32)
    moved_ref[n : 2 * n] = unit(n)
    moved_ref[2 * n :] = jnp.zeros((VECTOR, n), jnp.float32)
    waiting_ref[...] = jnp.zeros_like(waiting_ref)
    inverse_ref[...] = jnp.zeros_like(inverse_ref)
    info_ref[...] = jnp.zeros_like(info_ref)

    def through_sensed(spread):
        half = join_nt(left_moving(spread), right_ref[n:])
        return join_nn(left_ref[n:], right_moving(half))

    sensed_ref[...] = first_spread(
        0, jnp.where(begin == 0, through_sensed(prior_ref[...]), 0.0)
    )

    def update():
        white = join_nt(waiting_ref[...], inverse_ref[...])
        left = left_of(white)
        info_ref[...] = info_ref[...] + join_nt(left[n:], right_of(white[n : 2 * n]))
        return moved_ref[...] - join_nt(left, right_of(white[0:n]))

    def step(k, carry):
        ((_, inverse),) = factor_small([sensed_ref[...]], board, o // ROWS)
        now = wrap(begin + k)
        later = wrap(now + 1)
        state = update()
        state = jnp.where(
            now == 0,
            jnp.concatenate(
                [prior_ref[...], jnp.zeros((n, n), jnp.float32), first_of(mean_ref[...])], axis=0
            ),
            state,
        )
        moved = join_nt(left_moving(state), right_ref[...])
        ahead = join_nn(left_ref[0:n], right_moving(moved[0:n])) + consts_ref[0:n]
        moved_ref[0:n] = ahead[:, 0:n]
        moved_ref[n:] = moved[n:, 0:n]
        waiting_ref[0:n] = left_of(ahead[:, n:])
        waiting_ref[n : 2 * n] = left_of(moved[n : 2 * n, n:])
        waiting_ref[2 * n :] = left_of(moved[2 * n :, n:] - first_of(line_at(k)[:, 0:o]))
        kept = through_sensed(jnp.where(later == 0, prior_ref[...], ahead[:, 0:n]))
        gained = exact_nt(join_nn(left_ref[n:], right_moving(ahead[:, n:])), inverse)
        gained = jnp.where(later == 0, 0.0, gained)
        sensed_ref[...] = first_spread(k + 1, kept - exact_nt(gained, gained))
        inverse_ref[...] = right_of(inverse)
        return carry

    lax.fori_loop(0, steps, step, 0)
    state_ref[...] = update()


def meet_kernel(
    role_ref, state_ref, info_ref, far_state_ref, far_info_ref, mean_ref, cov_ref, board
):
    n = state_ref.shape[1]
    late = role_ref[0] == 1
    eye = unit(n)

    def of_cut(rows, near, far):
        return jnp.where(late, far[rows], near[rows])

    def of_middle(rows, near, far):
        return jnp.where(late, near[rows], far[rows])

    spread_rows, move_rows, center_rows = slice(0, n), slice(n, 2 * n), slice(2 * n, 2 * n + VECTOR)
    info_rows, vector_rows = slice(0, n), slice(n, n + VECTOR)
    cut_spread = of_cut(spread_rows, state_ref, far_state_ref)
    cut_center = of_cut(center_rows, state_ref, far_state_ref)
    cut_info = of_cut(info_rows, info_ref, far_info_ref)
    cut_vector = of_cut(vector_rows, info_ref, far_info_ref)
    mid_spread = of_middle(spread_rows, state_ref, far_state_ref)
    move = of_middle(move_rows, state_ref, far_state_ref)
    mid_center = of_middle(center_rows, state_ref, far_state_ref)
    mid_info = of_middle(info_rows, info_ref, far_info_ref)
    mid_vector = of_middle(vector_rows, info_ref, far_info_ref)

    (mid_root, _), (cut_root, _) = factor([mid_spread, cut_spread], board)
    rooted = exact_nt(cut_info, mid_root)
    ((_, inner),) = factor([eye + exact_nn(mid_root, rooted)], board)
    carried = near_nn(inner, mid_root)
    mixing = near_nt(rooted, inner)
    kept = cut_info - near_nt(mixing, mixing)
    early_info = mid_info + near_nt(near_nn(move, kept), move)
    ((_, last),) = factor(
        [eye + exact_nn(cut_root, exact_nt(early_info, cut_root))], board
    )
    residue = -cut_vector - near_nn(mid_center, cut_info)
    residue_carried = near_nt(residue, carried)
    early_vector = near_nt(residue - near_nt(residue_carried, mixing), move) - mid_vector
    pull = early_vector - near_nn(cut_center, early_info)
    cut_root_t = cut_root.T
    through = move - near_nn(near_nn(move, mixing), carried)
    through_center = mid_center + near_nn(residue_carried, carried)
    carried_t = carried.T
    leftover = near_nt(carried_t, carried_t)
    late_root = near_nt(through.T, cut_root)
    early_root = near_nt(cut_root_t, last)
    early_center = cut_center + near_nt(near_nn(pull, early_root), early_root)
    root = near_nt(jnp.where(late, late_root, cut_root_t), last)
    cov_ref[0] = jnp.where(late, leftover, 0.0) + near_nt(root, root)
    late_center = near_nn(early_center, through) + through_center
    mean_ref[...] = jnp.where(late, late_center, early_center)[0:1]


def begin_of(device, devices):
    quarter = devices // 4
    chip = device // 2
    upper = chip // quarter
    split = 2 * (chip - quarter * upper) + upper
    role = device % 2
    return (split + 1 + (1 - role) * (devices - devices // 2)) % devices


def gather_rows(rows, steps, axis):
    devices = lax.axis_size(axis)
    begins = [begin_of(i, devices) for i in range(devices)]
    holder = {begin: i for i, begin in enumerate(begins)}
    held = min(FAN, steps)
    parts = [
        lax.ppermute(rows, axis, [((begins[i] + j) % devices, i) for i in range(devices)])
        for j in range(held)
    ]
    rows = jnp.concatenate(parts, axis=0)
    while held < steps:
        parts = [rows]
        for m in range(1, FAN):
            size = min(held, steps - m * held)
            if size > 0:
                pairs = [(holder[(begins[i] + m * held) % devices], i) for i in range(devices)]
                parts.append(lax.ppermute(rows[:size], axis, pairs))
        rows = jnp.concatenate(parts, axis=0)
        held = min(steps, FAN * held)
    return rows


def shards(
    measurements, noise_levels, transition, sensing, process_noise, prior_mean, prior_covariance
):
    n = transition.shape[0]
    o = sensing.shape[0]
    devices = lax.axis_size("tm")
    half = devices // 2
    device = lax.axis_index("tm").astype(jnp.int32)
    role = device % 2
    begin = begin_of(device, devices)

    rows = gather_rows(jnp.concatenate([measurements, noise_levels], axis=1), half, "tm")
    vmem = pl.BlockSpec(memory_space=pltpu.VMEM)
    smem = pl.BlockSpec(memory_space=pltpu.SMEM)
    params = pltpu.CompilerParams(vmem_limit_bytes=48 * 1024 * 1024)

    def shape(*dims):
        return jax.ShapeDtypeStruct(dims, jnp.float32)

    passes = jax.ShapeDtypeStruct((n + o, 4 * n), jnp.bfloat16)
    left, right, consts = pl.pallas_call(
        maps_kernel,
        out_shape=(passes, passes, shape(n + o, n + o)),
        in_specs=[vmem] * 3,
        out_specs=(vmem, vmem, vmem),
        compiler_params=params,
    )(transition, sensing, process_noise)
    state, info = pl.pallas_call(
        functools.partial(window_kernel, half, devices),
        out_shape=(shape(2 * n + VECTOR, n), shape(n + VECTOR, n)),
        in_specs=[smem] + [vmem] * 6,
        out_specs=(vmem, vmem),
        scratch_shapes=[
            pltpu.VMEM((2 * n + VECTOR, n), jnp.float32),
            pltpu.VMEM((2 * n + VECTOR, 3 * o), jnp.bfloat16),
            pltpu.VMEM((o, 3 * o), jnp.bfloat16),
            pltpu.VMEM((o, o), jnp.float32),
            pltpu.VMEM((1, 2, BOARD, o), jnp.float32),
        ],
        compiler_params=params,
    )(begin.reshape(1), rows, left, right, consts, prior_mean.reshape(1, n), prior_covariance)
    swap = [(i, i ^ 1) for i in range(devices)]
    far_state = lax.ppermute(state, "tm", swap)
    far_info = lax.ppermute(info, "tm", swap)
    mean, cov = pl.pallas_call(
        meet_kernel,
        out_shape=(shape(1, n), shape(1, n, n)),
        in_specs=[smem] + [vmem] * 4,
        out_specs=(vmem, vmem),
        scratch_shapes=[pltpu.VMEM((2, 2, BOARD, LANES), jnp.float32)],
        compiler_params=params,
    )(role.reshape(1), state, info, far_state, far_info)
    home = []
    for i in range(devices):
        above = i >= half
        spot = 2 * ((i - half if above else i) // 2) + (1 if above else 0)
        home.append((i, spot + half if i % 2 else spot))
    return lax.ppermute(mean, "tm", home), lax.ppermute(cov, "tm", home)


def solution(mesh):
    return jax.shard_map(
        shards,
        mesh=mesh,
        in_specs=(P("tm", None), P("tm", None), P(), P(), P(), P(), P()),
        out_specs=(P("tm", None), P("tm", None, None)),
        check_vma=False,
    )
```

```python
import functools

import jax
import jax.numpy as jnp
from jax import lax
from jax.experimental import pallas as pl
from jax.experimental.pallas import tpu as pltpu
from jax.sharding import PartitionSpec as P

ROWS = 8
LANES = 128
VECTOR = 16
EXTRA = ROWS + ROWS // 2
BOARD = ROWS * (EXTRA + ROWS)
FAN = 4


def dot_nn(left, right):
    return lax.dot_general(
        left,
        right,
        (((1,), (0,)), ((), ())),
        precision=lax.Precision.HIGHEST,
        preferred_element_type=jnp.float32,
    )


def dot_nt(left, right):
    return lax.dot_general(
        left,
        right,
        (((1,), (1,)), ((), ())),
        precision=lax.Precision.HIGHEST,
        preferred_element_type=jnp.float32,
    )


def pieces(x, count):
    out = []
    for _ in range(count):
        out.append(x.astype(jnp.bfloat16))
        x = x - out[-1].astype(jnp.float32)
    return out


def left_of(x):
    high, low = pieces(x, 2)
    return jnp.concatenate([high, low, high], axis=1)


def right_of(x):
    high, low = pieces(x, 2)
    return jnp.concatenate([high, high, low], axis=1)


def left_moving(x):
    high, low = pieces(x, 2)
    return jnp.concatenate([high, low, high, high], axis=1)


def right_moving(x):
    high, low = pieces(x, 2)
    return jnp.concatenate([high, high, high, low], axis=0)


def join_nn(left, right):
    return lax.dot_general(
        left, right, (((1,), (0,)), ((), ())), preferred_element_type=jnp.float32
    )


def join_nt(left, right):
    return lax.dot_general(
        left, right, (((1,), (1,)), ((), ())), preferred_element_type=jnp.float32
    )


def spread_lane(x, lane):
    return jnp.broadcast_to(x[:, lane : lane + 1], x.shape)


def exact_nt(left, right):
    a, b, c = pieces(left, 3)
    p, q, r = pieces(right, 3)
    return join_nt(
        jnp.concatenate([a, a, b, a, b, c], axis=1), jnp.concatenate([p, q, p, r, q, p], axis=1)
    )


def exact_nn(left, right):
    a, b, c = pieces(left, 3)
    p, q, r = pieces(right, 3)
    return join_nn(
        jnp.concatenate([a, a, b, a, b, c], axis=1), jnp.concatenate([p, q, p, r, q, p], axis=0)
    )


def near_nn(left, right):
    high, low = pieces(right, 2)
    return join_nn(left_of(left), jnp.concatenate([high, high, low], axis=0))


def near_nt(left, right):
    return join_nt(left_of(left), right_of(right))


def factor_small(matrices, board):
    side = matrices[0].shape[0]
    count = side // ROWS
    shape = (ROWS, side)
    row = lax.broadcasted_iota(jnp.int32, shape, 0)
    lane = lax.broadcasted_iota(jnp.int32, shape, 1)
    tasks = [[m[ROWS * k : ROWS * (k + 1)] for k in range(count)] for m in matrices]
    outs = [([], []) for m in matrices]
    heads = [[spread_lane(X[0], i) for i in range(ROWS)] for X in tasks]
    for k in range(count):
        base = ROWS * k
        more = k + 1 < count
        for t, (X, out) in enumerate(zip(tasks, outs)):

            def put(slot, values):
                board[t, k % 2, ROWS * slot : ROWS * (slot + 1)] = values

            def spread(slot, r):
                at = ROWS * slot + r
                return jnp.broadcast_to(board[t, k % 2, at : at + 1], shape)

            cols = heads[t]
            for i in range(ROWS):
                put(i, cols[i])
            block = {(r, i): spread(i, r) for i in range(ROWS) for r in range(i, ROWS)}
            nexts = [spread_lane(X[k + 1], base + i) for i in range(ROWS)] if more else []
            heads[t] = [spread_lane(X[k + 1], base + ROWS + i) for i in range(ROWS)] if more else []
            pivots = jnp.ones(shape, jnp.float32)
            for i in range(0, ROWS, 2):
                p = base + i
                pair = (lane == p) | (lane == p + 1)
                a, b, c = block[i, i], block[i + 1, i], block[i + 1, i + 1]
                det = a * c - b * b
                ra = pltpu.reciprocal(a, approx=True)
                rdet = pltpu.reciprocal(det, approx=True)
                ratio = b * ra
                rest = range(i + 2, ROWS)
                firsts = {q: block[q, i] for q in rest}
                mixed = {q: a * block[q, i + 1] - b * firsts[q] for q in rest}
                seconds = {q: mixed[q] * ra for q in rest}
                for q in rest:
                    for r in range(q, ROWS):
                        block[r, q] = (
                            block[r, q] - (firsts[r] * ra) * firsts[q] - (mixed[r] * rdet) * seconds[q]
                        )
                pivots = jnp.where(row == i, a, pivots)
                pivots = jnp.where(row == i + 1, det * ra, pivots)
                put(ROWS + i // 2, X[k])
                xp = spread(ROWS + i // 2, i)
                xp = jnp.where(lane == p, 1.0, jnp.where(lane == p + 1, 0.0, xp))
                xq = spread(ROWS + i // 2, i + 1)
                xq = jnp.where(lane == p + 1, 1.0, jnp.where(lane == p, 0.0, xq))
                xq = xq - ratio * xp
                xp_scaled = xp * ra
                xq_scaled = xq * (a * rdet)
                Z = jnp.where((row == i) & (lane == p), 1.0, X[k])
                if i + 2 < ROWS:
                    f0 = cols[i] * ra
                    f1 = (a * cols[i + 1] - b * cols[i]) * rdet
                    for q in rest:
                        cols[q] = cols[q] - f0 * firsts[q] - f1 * seconds[q]
                    m0 = jnp.where(row > i + 1, f0, 0.0)
                    m1 = jnp.where(row > i + 1, f1, 0.0)
                    Z = jnp.where((row > i + 1) & pair, 0.0, Z) - m0 * xp - m1 * xq
                X[k] = jnp.where(row == i + 1, xq, Z)
                if more:
                    g0, g1 = nexts[i], nexts[i + 1]
                    h0 = g0 * ra
                    g1 = a * g1 - b * g0
                    h1 = g1 * rdet
                    put(EXTRA + i, g0)
                    put(EXTRA + i + 1, g1 * ra)
                    for q in range(ROWS):
                        first, second = spread(EXTRA + i, q), spread(EXTRA + i + 1, q)
                        heads[t][q] = heads[t][q] - h0 * first - h1 * second
                    for q in rest:
                        nexts[q] = nexts[q] - h0 * firsts[q] - h1 * seconds[q]
                    X[k + 1] = jnp.where(pair, 0.0, X[k + 1]) - h0 * xp - h1 * xq
                for j in range(k + 2, count):
                    g0 = spread_lane(X[j], p)
                    g1 = spread_lane(X[j], p + 1) - ratio * g0
                    X[j] = jnp.where(pair, 0.0, X[j]) - g0 * xp_scaled - g1 * xq_scaled
            s = lax.rsqrt(pivots)
            s = s * (1.5 - 0.5 * pivots * s * s)
            scaled = X[k] * s
            diagonal = jnp.where(lane == row + base, pivots * s, 0.0)
            out[0].append(jnp.where(lane > row + base, scaled, diagonal))
            out[1].append(jnp.where(lane <= row + base, scaled, 0.0))
    return [(jnp.concatenate(u, axis=0), jnp.concatenate(v, axis=0)) for u, v in outs]


def factor(matrices, board):
    blocks = matrices[0].shape[0] // LANES
    if blocks == 1:
        return factor_small(matrices, board)

    def cut(m, i, j):
        return m[LANES * i : LANES * (i + 1), LANES * j : LANES * (j + 1)]

    zero = jnp.zeros((LANES, LANES), jnp.float32)
    uppers = [{} for m in matrices]
    lowers = [{} for m in matrices]
    inverses = [{} for m in matrices]
    for j in range(blocks):
        heads = []
        for m, U, L in zip(matrices, uppers, lowers):
            head = cut(m, j, j)
            for k in range(j):
                head = head - exact_nt(L[j, k], L[j, k])
            heads.append(head)
        for m, U, L, V, (u, v) in zip(
            matrices, uppers, lowers, inverses, factor_small(heads, board)
        ):
            U[j, j] = u
            V[j, j] = v
            for i in range(j + 1, blocks):
                right = cut(m, j, i)
                down = cut(m, i, j)
                for k in range(j):
                    right = right - exact_nn(L[j, k], U[k, i])
                    down = down - exact_nn(L[i, k], U[k, j])
                U[j, i] = exact_nn(v, right)
                L[i, j] = exact_nt(down, v)
    outs = []
    for U, L, V in zip(uppers, lowers, inverses):
        for i in range(blocks):
            for j in range(i):
                total = exact_nn(L[i, j], V[j, j])
                for k in range(j + 1, i):
                    total = total + exact_nn(L[i, k], V[k, j])
                V[i, j] = -exact_nn(V[i, i], total)
        whole = [
            jnp.concatenate(
                [
                    jnp.concatenate([D.get((i, j), zero) for j in range(blocks)], axis=1)
                    for i in range(blocks)
                ],
                axis=0,
            )
            for D in (U, V)
        ]
        outs.append(tuple(whole))
    return outs


def unit(side):
    row = lax.broadcasted_iota(jnp.int32, (side, side), 0)
    col = lax.broadcasted_iota(jnp.int32, (side, side), 1)
    return jnp.where(row == col, 1.0, 0.0)


def first_of(values):
    row = lax.broadcasted_iota(jnp.int32, (VECTOR, values.shape[1]), 0)
    return jnp.where(row == 0, values, 0.0)


def maps_kernel(transition_ref, sensing_ref, noise_ref, left_ref, right_ref, consts_ref):
    n = transition_ref.shape[0]
    transition = transition_ref[...]
    sensing = sensing_ref[...]
    noise = noise_ref[...]
    maps = jnp.concatenate([transition, dot_nn(sensing, transition)], axis=0)
    high, low, least = pieces(maps, 3)
    left_ref[...] = jnp.concatenate([high, low, least, high], axis=1)
    right_ref[...] = jnp.concatenate([high, high, low, least], axis=1)
    noise_sensed = dot_nt(noise, sensing)
    consts_ref[0:n, 0:n] = noise
    consts_ref[0:n, n:] = noise_sensed
    consts_ref[n:, 0:n] = jnp.zeros((sensing.shape[0], n), jnp.float32)
    consts_ref[n:, n:] = dot_nn(sensing, noise_sensed)


def window_kernel(
    steps,
    times,
    begin_ref,
    rows_ref,
    left_ref,
    right_ref,
    consts_ref,
    mean_ref,
    prior_ref,
    state_ref,
    info_ref,
    moved_ref,
    waiting_ref,
    inverse_ref,
    sensed_ref,
    board,
):
    n = prior_ref.shape[0]
    o = left_ref.shape[0] - n
    begin = begin_ref[0]
    eye_sense = unit(o)

    def wrap(t):
        return jnp.where(t >= times, t - times, t)

    def line_at(k):
        return rows_ref[pl.ds(jnp.minimum(k, steps - 1), 1), :]

    def first_spread(k, spread):
        line = line_at(k)
        return spread + consts_ref[n:, n:] + eye_sense * line[:, o:]

    moved_ref[0:n] = jnp.zeros((n, n), jnp.float32)
    moved_ref[n : 2 * n] = unit(n)
    moved_ref[2 * n :] = jnp.zeros((VECTOR, n), jnp.float32)
    waiting_ref[...] = jnp.zeros_like(waiting_ref)
    inverse_ref[...] = jnp.zeros_like(inverse_ref)
    info_ref[...] = jnp.zeros_like(info_ref)

    def through_sensed(spread):
        half = join_nt(left_moving(spread), right_ref[n:])
        return join_nn(left_ref[n:], right_moving(half))

    sensed_ref[...] = first_spread(
        0, jnp.where(begin == 0, through_sensed(prior_ref[...]), 0.0)
    )

    def update():
        white = join_nt(waiting_ref[...], inverse_ref[...])
        left = left_of(white)
        info_ref[...] = info_ref[...] + join_nt(left[n:], right_of(white[n : 2 * n]))
        return moved_ref[...] - join_nt(left, right_of(white[0:n]))

    def step(k, carry):
        ((_, inverse),) = factor_small([sensed_ref[...]], board)
        now = wrap(begin + k)
        later = wrap(now + 1)
        state = update()
        state = jnp.where(
            now == 0,
            jnp.concatenate(
                [prior_ref[...], jnp.zeros((n, n), jnp.float32), first_of(mean_ref[...])], axis=0
            ),
            state,
        )
        moved = join_nt(left_moving(state), right_ref[...])
        ahead = join_nn(left_ref[0:n], right_moving(moved[0:n])) + consts_ref[0:n]
        moved_ref[0:n] = ahead[:, 0:n]
        moved_ref[n:] = moved[n:, 0:n]
        waiting_ref[0:n] = left_of(ahead[:, n:])
        waiting_ref[n : 2 * n] = left_of(moved[n : 2 * n, n:])
        waiting_ref[2 * n :] = left_of(moved[2 * n :, n:] - first_of(line_at(k)[:, 0:o]))
        kept = through_sensed(jnp.where(later == 0, prior_ref[...], ahead[:, 0:n]))
        gained = exact_nt(join_nn(left_ref[n:], right_moving(ahead[:, n:])), inverse)
        gained = jnp.where(later == 0, 0.0, gained)
        sensed_ref[...] = first_spread(k + 1, kept - exact_nt(gained, gained))
        inverse_ref[...] = right_of(inverse)
        return carry

    lax.fori_loop(0, steps, step, 0)
    state = update()
    ((root, _),) = factor([state[0:n]], board)
    state_ref[0:n] = root
    state_ref[n:] = state[n:]


def meet_kernel(
    role_ref, state_ref, info_ref, far_state_ref, far_info_ref, mean_ref, cov_ref, board
):
    n = state_ref.shape[1]
    late = role_ref[0] == 1
    eye = unit(n)

    def of_cut(rows, near, far):
        return jnp.where(late, far[rows], near[rows])

    def of_middle(rows, near, far):
        return jnp.where(late, near[rows], far[rows])

    root_rows, move_rows, center_rows = slice(0, n), slice(n, 2 * n), slice(2 * n, 2 * n + VECTOR)
    info_rows, vector_rows = slice(0, n), slice(n, n + VECTOR)
    cut_root = of_cut(root_rows, state_ref, far_state_ref)
    cut_center = of_cut(center_rows, state_ref, far_state_ref)
    cut_info = of_cut(info_rows, info_ref, far_info_ref)
    cut_vector = of_cut(vector_rows, info_ref, far_info_ref)
    mid_root = of_middle(root_rows, state_ref, far_state_ref)
    move = of_middle(move_rows, state_ref, far_state_ref)
    mid_center = of_middle(center_rows, state_ref, far_state_ref)
    mid_info = of_middle(info_rows, info_ref, far_info_ref)
    mid_vector = of_middle(vector_rows, info_ref, far_info_ref)

    rooted = exact_nt(cut_info, mid_root)
    ((_, inner),) = factor([eye + exact_nn(mid_root, rooted)], board)
    carried = near_nn(inner, mid_root)
    mixing = near_nt(rooted, inner)
    kept = cut_info - near_nt(mixing, mixing)
    early_info = mid_info + near_nt(near_nn(move, kept), move)
    ((_, last),) = factor(
        [eye + exact_nn(cut_root, exact_nt(early_info, cut_root))], board
    )
    residue = -cut_vector - near_nn(mid_center, cut_info)
    residue_carried = near_nt(residue, carried)
    early_vector = near_nt(residue - near_nt(residue_carried, mixing), move) - mid_vector
    pull = early_vector - near_nn(cut_center, early_info)
    cut_root_t = cut_root.T
    through = move - near_nn(near_nn(move, mixing), carried)
    through_center = mid_center + near_nn(residue_carried, carried)
    carried_t = carried.T
    leftover = near_nt(carried_t, carried_t)
    late_root = near_nt(through.T, cut_root)
    early_root = near_nt(cut_root_t, last)
    early_center = cut_center + near_nt(near_nn(pull, early_root), early_root)
    root = near_nt(jnp.where(late, late_root, cut_root_t), last)
    cov_ref[0] = jnp.where(late, leftover, 0.0) + near_nt(root, root)
    late_center = near_nn(early_center, through) + through_center
    mean_ref[...] = jnp.where(late, late_center, early_center)[0:1]


def begin_of(device, devices):
    quarter = devices // 4
    chip = device // 2
    upper = chip // quarter
    split = 2 * (chip - quarter * upper) + upper
    role = device % 2
    return (split + 1 + (1 - role) * (devices - devices // 2)) % devices


def gather_rows(rows, steps, axis):
    devices = lax.axis_size(axis)
    begins = [begin_of(i, devices) for i in range(devices)]
    holder = {begin: i for i, begin in enumerate(begins)}
    held = min(FAN, steps)
    parts = [
        lax.ppermute(rows, axis, [((begins[i] + j) % devices, i) for i in range(devices)])
        for j in range(held)
    ]
    rows = jnp.concatenate(parts, axis=0)
    while held < steps:
        parts = [rows]
        for m in range(1, FAN):
            size = min(held, steps - m * held)
            if size > 0:
                pairs = [(holder[(begins[i] + m * held) % devices], i) for i in range(devices)]
                parts.append(lax.ppermute(rows[:size], axis, pairs))
        rows = jnp.concatenate(parts, axis=0)
        held = min(steps, FAN * held)
    return rows


def shards(
    measurements, noise_levels, transition, sensing, process_noise, prior_mean, prior_covariance
):
    n = transition.shape[0]
    o = sensing.shape[0]
    devices = lax.axis_size("tm")
    half = devices // 2
    device = lax.axis_index("tm").astype(jnp.int32)
    role = device % 2
    begin = begin_of(device, devices)

    rows = gather_rows(jnp.concatenate([measurements, noise_levels], axis=1), half, "tm")
    vmem = pl.BlockSpec(memory_space=pltpu.VMEM)
    smem = pl.BlockSpec(memory_space=pltpu.SMEM)
    params = pltpu.CompilerParams(vmem_limit_bytes=48 * 1024 * 1024)

    def shape(*dims):
        return jax.ShapeDtypeStruct(dims, jnp.float32)

    passes = jax.ShapeDtypeStruct((n + o, 4 * n), jnp.bfloat16)
    left, right, consts = pl.pallas_call(
        maps_kernel,
        out_shape=(passes, passes, shape(n + o, n + o)),
        in_specs=[vmem] * 3,
        out_specs=(vmem, vmem, vmem),
        compiler_params=params,
    )(transition, sensing, process_noise)
    state, info = pl.pallas_call(
        functools.partial(window_kernel, half, devices),
        out_shape=(shape(2 * n + VECTOR, n), shape(n + VECTOR, n)),
        in_specs=[smem] + [vmem] * 6,
        out_specs=(vmem, vmem),
        scratch_shapes=[
            pltpu.VMEM((2 * n + VECTOR, n), jnp.float32),
            pltpu.VMEM((2 * n + VECTOR, 3 * o), jnp.bfloat16),
            pltpu.VMEM((o, 3 * o), jnp.bfloat16),
            pltpu.VMEM((o, o), jnp.float32),
            pltpu.VMEM((1, 2, BOARD, o), jnp.float32),
        ],
        compiler_params=params,
    )(begin.reshape(1), rows, left, right, consts, prior_mean.reshape(1, n), prior_covariance)
    swap = [(i, i ^ 1) for i in range(devices)]
    far_state = lax.ppermute(state, "tm", swap)
    far_info = lax.ppermute(info, "tm", swap)
    mean, cov = pl.pallas_call(
        meet_kernel,
        out_shape=(shape(1, n), shape(1, n, n)),
        in_specs=[smem] + [vmem] * 4,
        out_specs=(vmem, vmem),
        scratch_shapes=[pltpu.VMEM((1, 2, BOARD, LANES), jnp.float32)],
        compiler_params=params,
    )(role.reshape(1), state, info, far_state, far_info)
    home = []
    for i in range(devices):
        above = i >= half
        spot = 2 * ((i - half if above else i) // 2) + (1 if above else 0)
        home.append((i, spot + half if i % 2 else spot))
    return lax.ppermute(mean, "tm", home), lax.ppermute(cov, "tm", home)


def solution(mesh):
    return jax.shard_map(
        shards,
        mesh=mesh,
        in_specs=(P("tm", None), P("tm", None), P(), P(), P(), P(), P()),
        out_specs=(P("tm", None), P("tm", None, None)),
        check_vma=False,
    )
```

```python
import functools

import jax
import jax.numpy as jnp
from jax import lax
from jax.experimental import pallas as pl
from jax.experimental.pallas import tpu as pltpu
from jax.sharding import PartitionSpec as P

ROWS = 8
LANES = 128
VECTOR = 16
EXTRA = ROWS + ROWS // 2
BOARD = ROWS * (EXTRA + ROWS)
FAN = 4


def pieces(x, count):
    out = []
    for _ in range(count):
        out.append(x.astype(jnp.bfloat16))
        x = x - out[-1].astype(jnp.float32)
    return out


def left_of(x):
    high, low = pieces(x, 2)
    return jnp.concatenate([high, low, high], axis=1)


def right_of(x):
    high, low = pieces(x, 2)
    return jnp.concatenate([high, high, low], axis=1)


def left_moving(x):
    high, low = pieces(x, 2)
    return jnp.concatenate([high, low, high, high], axis=1)


def right_moving(x):
    high, low = pieces(x, 2)
    return jnp.concatenate([high, high, high, low], axis=0)


def join_nn(left, right):
    return lax.dot_general(
        left, right, (((1,), (0,)), ((), ())), preferred_element_type=jnp.float32
    )


def join_nt(left, right):
    return lax.dot_general(
        left, right, (((1,), (1,)), ((), ())), preferred_element_type=jnp.float32
    )


def spread_lane(x, lane):
    return jnp.broadcast_to(x[:, lane : lane + 1], x.shape)


def exact_nt(left, right):
    a, b, c = pieces(left, 3)
    p, q, r = pieces(right, 3)
    return join_nt(
        jnp.concatenate([a, a, b, a, b, c], axis=1), jnp.concatenate([p, q, p, r, q, p], axis=1)
    )


def exact_nn(left, right):
    a, b, c = pieces(left, 3)
    p, q, r = pieces(right, 3)
    return join_nn(
        jnp.concatenate([a, a, b, a, b, c], axis=1), jnp.concatenate([p, q, p, r, q, p], axis=0)
    )


def near_nn(left, right):
    high, low = pieces(right, 2)
    return join_nn(left_of(left), jnp.concatenate([high, high, low], axis=0))


def near_nt(left, right):
    return join_nt(left_of(left), right_of(right))


def factor_small(matrices, board):
    side = matrices[0].shape[0]
    count = side // ROWS
    shape = (ROWS, side)
    row = lax.broadcasted_iota(jnp.int32, shape, 0)
    lane = lax.broadcasted_iota(jnp.int32, shape, 1)
    tasks = [[m[ROWS * k : ROWS * (k + 1)] for k in range(count)] for m in matrices]
    outs = [([], []) for m in matrices]
    heads = [[spread_lane(X[0], i) for i in range(ROWS)] for X in tasks]
    for k in range(count):
        base = ROWS * k
        more = k + 1 < count
        for t, (X, out) in enumerate(zip(tasks, outs)):

            def put(slot, values):
                board[t, k % 2, ROWS * slot : ROWS * (slot + 1)] = values

            def spread(slot, r):
                at = ROWS * slot + r
                return jnp.broadcast_to(board[t, k % 2, at : at + 1], shape)

            cols = heads[t]
            for i in range(ROWS):
                put(i, cols[i])
            block = {(r, i): spread(i, r) for i in range(ROWS) for r in range(i, ROWS)}
            nexts = [spread_lane(X[k + 1], base + i) for i in range(ROWS)] if more else []
            heads[t] = [spread_lane(X[k + 1], base + ROWS + i) for i in range(ROWS)] if more else []
            pivots = jnp.ones(shape, jnp.float32)
            for i in range(0, ROWS, 2):
                p = base + i
                pair = (lane == p) | (lane == p + 1)
                a, b, c = block[i, i], block[i + 1, i], block[i + 1, i + 1]
                det = a * c - b * b
                ra = pltpu.reciprocal(a, approx=True)
                rdet = pltpu.reciprocal(det, approx=True)
                ratio = b * ra
                rest = range(i + 2, ROWS)
                firsts = {q: block[q, i] for q in rest}
                mixed = {q: a * block[q, i + 1] - b * firsts[q] for q in rest}
                seconds = {q: mixed[q] * ra for q in rest}
                for q in rest:
                    for r in range(q, ROWS):
                        block[r, q] = (
                            block[r, q] - (firsts[r] * ra) * firsts[q] - (mixed[r] * rdet) * seconds[q]
                        )
                pivots = jnp.where(row == i, a, pivots)
                pivots = jnp.where(row == i + 1, det * ra, pivots)
                put(ROWS + i // 2, X[k])
                xp = spread(ROWS + i // 2, i)
                xp = jnp.where(lane == p, 1.0, jnp.where(lane == p + 1, 0.0, xp))
                xq = spread(ROWS + i // 2, i + 1)
                xq = jnp.where(lane == p + 1, 1.0, jnp.where(lane == p, 0.0, xq))
                xq = xq - ratio * xp
                xp_scaled = xp * ra
                xq_scaled = xq * (a * rdet)
                Z = jnp.where((row == i) & (lane == p), 1.0, X[k])
                if i + 2 < ROWS:
                    f0 = cols[i] * ra
                    f1 = (a * cols[i + 1] - b * cols[i]) * rdet
                    for q in rest:
                        cols[q] = cols[q] - f0 * firsts[q] - f1 * seconds[q]
                    m0 = jnp.where(row > i + 1, f0, 0.0)
                    m1 = jnp.where(row > i + 1, f1, 0.0)
                    Z = jnp.where((row > i + 1) & pair, 0.0, Z) - m0 * xp - m1 * xq
                X[k] = jnp.where(row == i + 1, xq, Z)
                if more:
                    g0, g1 = nexts[i], nexts[i + 1]
                    h0 = g0 * ra
                    g1 = a * g1 - b * g0
                    h1 = g1 * rdet
                    put(EXTRA + i, g0)
                    put(EXTRA + i + 1, g1 * ra)
                    for q in range(ROWS):
                        first, second = spread(EXTRA + i, q), spread(EXTRA + i + 1, q)
                        heads[t][q] = heads[t][q] - h0 * first - h1 * second
                    for q in rest:
                        nexts[q] = nexts[q] - h0 * firsts[q] - h1 * seconds[q]
                    X[k + 1] = jnp.where(pair, 0.0, X[k + 1]) - h0 * xp - h1 * xq
                for j in range(k + 2, count):
                    g0 = spread_lane(X[j], p)
                    g1 = spread_lane(X[j], p + 1) - ratio * g0
                    X[j] = jnp.where(pair, 0.0, X[j]) - g0 * xp_scaled - g1 * xq_scaled
            s = lax.rsqrt(pivots)
            s = s * (1.5 - 0.5 * pivots * s * s)
            scaled = X[k] * s
            diagonal = jnp.where(lane == row + base, pivots * s, 0.0)
            out[0].append(jnp.where(lane > row + base, scaled, diagonal))
            out[1].append(jnp.where(lane <= row + base, scaled, 0.0))
    return [(jnp.concatenate(u, axis=0), jnp.concatenate(v, axis=0)) for u, v in outs]


def factor(matrices, board):
    blocks = matrices[0].shape[0] // LANES
    if blocks == 1:
        return factor_small(matrices, board)

    def cut(m, i, j):
        return m[LANES * i : LANES * (i + 1), LANES * j : LANES * (j + 1)]

    zero = jnp.zeros((LANES, LANES), jnp.float32)
    uppers = [{} for m in matrices]
    lowers = [{} for m in matrices]
    inverses = [{} for m in matrices]
    for j in range(blocks):
        heads = []
        for m, U, L in zip(matrices, uppers, lowers):
            head = cut(m, j, j)
            for k in range(j):
                head = head - exact_nt(L[j, k], L[j, k])
            heads.append(head)
        for m, U, L, V, (u, v) in zip(
            matrices, uppers, lowers, inverses, factor_small(heads, board)
        ):
            U[j, j] = u
            V[j, j] = v
            for i in range(j + 1, blocks):
                right = cut(m, j, i)
                down = cut(m, i, j)
                for k in range(j):
                    right = right - exact_nn(L[j, k], U[k, i])
                    down = down - exact_nn(L[i, k], U[k, j])
                U[j, i] = exact_nn(v, right)
                L[i, j] = exact_nt(down, v)
    outs = []
    for U, L, V in zip(uppers, lowers, inverses):
        for i in range(blocks):
            for j in range(i):
                total = exact_nn(L[i, j], V[j, j])
                for k in range(j + 1, i):
                    total = total + exact_nn(L[i, k], V[k, j])
                V[i, j] = -exact_nn(V[i, i], total)
        whole = [
            jnp.concatenate(
                [
                    jnp.concatenate([D.get((i, j), zero) for j in range(blocks)], axis=1)
                    for i in range(blocks)
                ],
                axis=0,
            )
            for D in (U, V)
        ]
        outs.append(tuple(whole))
    return outs


def unit(side):
    row = lax.broadcasted_iota(jnp.int32, (side, side), 0)
    col = lax.broadcasted_iota(jnp.int32, (side, side), 1)
    return jnp.where(row == col, 1.0, 0.0)


def first_of(values):
    row = lax.broadcasted_iota(jnp.int32, (VECTOR, values.shape[1]), 0)
    return jnp.where(row == 0, values, 0.0)


def maps_kernel(
    transition_ref,
    sensing_ref,
    noise_ref,
    prior_ref,
    left_ref,
    right_ref,
    fresh_ref,
    sensed_noise_ref,
    sensed_fresh_ref,
):
    n = transition_ref.shape[0]
    o = sensing_ref.shape[0]
    transition = transition_ref[...]
    sensing = sensing_ref[...]
    noise = noise_ref[...]
    sensed = exact_nn(sensing, transition)
    maps = jnp.concatenate([transition, sensing, sensed], axis=0)
    high, low, least = pieces(maps, 3)
    right_ref[...] = jnp.concatenate([high, high, low, least], axis=1)
    left = jnp.concatenate([high, low, least, high], axis=1)
    left_ref[0:n] = left[0:n]
    left_ref[n:] = left[n + o :]
    sensed_noise_ref[...] = exact_nn(sensing, exact_nt(noise, sensing))
    carried = exact_nt(prior_ref[...], jnp.concatenate([transition, sensed], axis=0))
    fresh_ref[...] = exact_nn(transition, carried[:, 0:n]) + noise
    sensed_fresh_ref[...] = exact_nn(sensed, carried[:, n:])


def window_kernel(
    steps,
    times,
    begin_ref,
    rows_ref,
    left_ref,
    right_ref,
    noise_ref,
    fresh_ref,
    sensed_noise_ref,
    sensed_fresh_ref,
    mean_ref,
    state_ref,
    info_ref,
    spread_ref,
    before_ref,
    moved_ref,
    waiting_ref,
    inverse_ref,
    sensed_ref,
    board,
):
    n = noise_ref.shape[0]
    o = sensed_noise_ref.shape[0]
    begin = begin_ref[0]
    eye_sense = unit(o)

    def wrap(t):
        return jnp.where(t >= times, t - times, t)

    def line_at(k):
        return rows_ref[pl.ds(jnp.minimum(k, steps - 1), 1), :]

    def innovation(k, spread):
        return spread + sensed_noise_ref[...] + eye_sense * line_at(k)[:, o:]

    moved_ref[0:n] = unit(n)
    moved_ref[n:] = jnp.zeros((VECTOR, n), jnp.float32)
    waiting_ref[...] = jnp.zeros_like(waiting_ref)
    inverse_ref[...] = jnp.zeros_like(inverse_ref)
    info_ref[...] = jnp.zeros_like(info_ref)
    spread_ref[...] = jnp.where(begin == 0, fresh_ref[...], noise_ref[...])
    sensed_ref[...] = innovation(0, jnp.where(begin == 0, sensed_fresh_ref[...], 0.0))

    def update():
        white = join_nt(waiting_ref[...], inverse_ref[...])
        left = left_of(white[n:])
        info_ref[...] = info_ref[...] + join_nt(left, right_of(white[n : 2 * n]))
        return moved_ref[...] - join_nt(left, right_of(white[0:n])), white[0:n]

    def step(k, carry):
        ((_, inverse),) = factor_small([sensed_ref[...]], board)
        now = wrap(begin + k)
        renewed = wrap(now + 1) == 0
        spread = spread_ref[...]
        seen = join_nt(left_moving(spread), right_ref[...])
        ready = right_moving(seen)
        ahead = join_nn(left_ref[0:n], ready[:, 0 : n + o])
        sensed_ahead = join_nn(left_ref[n:], ready[:, n:])
        move, _ = update()
        move = jnp.where(
            now == 0,
            jnp.concatenate([jnp.zeros((n, n), jnp.float32), first_of(mean_ref[...])], axis=0),
            move,
        )
        move = left_moving(move)
        moved_ref[...] = join_nt(move, right_ref[0:n])
        errors = join_nt(move, right_ref[n + o :])
        waiting_ref[0:n] = left_of(seen[:, n : n + o])
        waiting_ref[n : 2 * n] = left_of(errors[0:n])
        waiting_ref[2 * n :] = left_of(errors[n:] - first_of(line_at(k)[:, 0:o]))
        before_ref[...] = spread
        gained = exact_nt(sensed_ahead[:, 0:o], inverse)
        sensed_ref[...] = innovation(
            k + 1,
            jnp.where(renewed, sensed_fresh_ref[...], sensed_ahead[:, o:] - exact_nt(gained, gained)),
        )
        inverse_right = right_of(inverse)
        inverse_ref[...] = inverse_right
        gain = join_nt(left_of(ahead[:, n:]), inverse_right)
        later = ahead[:, 0:n] + noise_ref[...] - join_nt(left_of(gain), right_of(gain))
        spread_ref[...] = jnp.where(renewed, fresh_ref[...], later)
        return carry

    lax.fori_loop(0, steps, step, 0)
    move, gain = update()
    ((root, _),) = factor([before_ref[...] - near_nt(gain, gain)], board)
    state_ref[0:n] = root
    state_ref[n:] = move


def meet_kernel(
    role_ref, state_ref, info_ref, far_state_ref, far_info_ref, mean_ref, cov_ref, board
):
    n = state_ref.shape[1]
    late = role_ref[0] == 1
    eye = unit(n)

    def of_cut(rows, near, far):
        return jnp.where(late, far[rows], near[rows])

    def of_middle(rows, near, far):
        return jnp.where(late, near[rows], far[rows])

    root_rows, move_rows, center_rows = slice(0, n), slice(n, 2 * n), slice(2 * n, 2 * n + VECTOR)
    info_rows, vector_rows = slice(0, n), slice(n, n + VECTOR)
    cut_root = of_cut(root_rows, state_ref, far_state_ref)
    cut_center = of_cut(center_rows, state_ref, far_state_ref)
    cut_info = of_cut(info_rows, info_ref, far_info_ref)
    cut_vector = of_cut(vector_rows, info_ref, far_info_ref)
    mid_root = of_middle(root_rows, state_ref, far_state_ref)
    move = of_middle(move_rows, state_ref, far_state_ref)
    mid_center = of_middle(center_rows, state_ref, far_state_ref)
    mid_info = of_middle(info_rows, info_ref, far_info_ref)
    mid_vector = of_middle(vector_rows, info_ref, far_info_ref)

    rooted = exact_nt(cut_info, mid_root)
    ((_, inner),) = factor([eye + exact_nn(mid_root, rooted)], board)
    carried = near_nn(inner, mid_root)
    mixing = near_nt(rooted, inner)
    kept = cut_info - near_nt(mixing, mixing)
    early_info = mid_info + near_nt(near_nn(move, kept), move)
    ((_, last),) = factor(
        [eye + exact_nn(cut_root, exact_nt(early_info, cut_root))], board
    )
    residue = -cut_vector - near_nn(mid_center, cut_info)
    residue_carried = near_nt(residue, carried)
    early_vector = near_nt(residue - near_nt(residue_carried, mixing), move) - mid_vector
    pull = early_vector - near_nn(cut_center, early_info)
    cut_root_t = cut_root.T
    through = move - near_nn(near_nn(move, mixing), carried)
    through_center = mid_center + near_nn(residue_carried, carried)
    carried_t = carried.T
    leftover = near_nt(carried_t, carried_t)
    late_root = near_nt(through.T, cut_root)
    early_root = near_nt(cut_root_t, last)
    early_center = cut_center + near_nt(near_nn(pull, early_root), early_root)
    root = near_nt(jnp.where(late, late_root, cut_root_t), last)
    cov_ref[0] = jnp.where(late, leftover, 0.0) + near_nt(root, root)
    late_center = near_nn(early_center, through) + through_center
    mean_ref[...] = jnp.where(late, late_center, early_center)[0:1]


def begin_of(device, devices):
    quarter = devices // 4
    chip = device // 2
    upper = chip // quarter
    split = 2 * (chip - quarter * upper) + upper
    role = device % 2
    return (split + 1 + (1 - role) * (devices - devices // 2)) % devices


def gather_rows(rows, steps, axis):
    devices = lax.axis_size(axis)
    begins = [begin_of(i, devices) for i in range(devices)]
    holder = {begin: i for i, begin in enumerate(begins)}
    held = min(FAN, steps)
    parts = [
        lax.ppermute(rows, axis, [((begins[i] + j) % devices, i) for i in range(devices)])
        for j in range(held)
    ]
    rows = jnp.concatenate(parts, axis=0)
    while held < steps:
        parts = [rows]
        for m in range(1, FAN):
            size = min(held, steps - m * held)
            if size > 0:
                pairs = [(holder[(begins[i] + m * held) % devices], i) for i in range(devices)]
                parts.append(lax.ppermute(rows[:size], axis, pairs))
        rows = jnp.concatenate(parts, axis=0)
        held = min(steps, FAN * held)
    return rows


def shards(
    measurements, noise_levels, transition, sensing, process_noise, prior_mean, prior_covariance
):
    n = transition.shape[0]
    o = sensing.shape[0]
    devices = lax.axis_size("tm")
    half = devices // 2
    device = lax.axis_index("tm").astype(jnp.int32)
    role = device % 2
    begin = begin_of(device, devices)

    rows = gather_rows(jnp.concatenate([measurements, noise_levels], axis=1), half, "tm")
    vmem = pl.BlockSpec(memory_space=pltpu.VMEM)
    smem = pl.BlockSpec(memory_space=pltpu.SMEM)
    params = pltpu.CompilerParams(vmem_limit_bytes=48 * 1024 * 1024)

    def shape(*dims):
        return jax.ShapeDtypeStruct(dims, jnp.float32)

    left, right, fresh, sensed_noise, sensed_fresh = pl.pallas_call(
        maps_kernel,
        out_shape=(
            jax.ShapeDtypeStruct((n + o, 4 * n), jnp.bfloat16),
            jax.ShapeDtypeStruct((n + 2 * o, 4 * n), jnp.bfloat16),
            shape(n, n),
            shape(o, o),
            shape(o, o),
        ),
        in_specs=[vmem] * 4,
        out_specs=(vmem,) * 5,
        compiler_params=params,
    )(transition, sensing, process_noise, prior_covariance)
    state, info = pl.pallas_call(
        functools.partial(window_kernel, half, devices),
        out_shape=(shape(2 * n + VECTOR, n), shape(n + VECTOR, n)),
        in_specs=[smem] + [vmem] * 8,
        out_specs=(vmem, vmem),
        scratch_shapes=[
            pltpu.VMEM((n, n), jnp.float32),
            pltpu.VMEM((n, n), jnp.float32),
            pltpu.VMEM((n + VECTOR, n), jnp.float32),
            pltpu.VMEM((2 * n + VECTOR, 3 * o), jnp.bfloat16),
            pltpu.VMEM((o, 3 * o), jnp.bfloat16),
            pltpu.VMEM((o, o), jnp.float32),
            pltpu.VMEM((1, 2, BOARD, o), jnp.float32),
        ],
        compiler_params=params,
    )(
        begin.reshape(1),
        rows,
        left,
        right,
        process_noise,
        fresh,
        sensed_noise,
        sensed_fresh,
        prior_mean.reshape(1, n),
    )
    swap = [(i, i ^ 1) for i in range(devices)]
    far_state = lax.ppermute(state, "tm", swap)
    far_info = lax.ppermute(info, "tm", swap)
    mean, cov = pl.pallas_call(
        meet_kernel,
        out_shape=(shape(1, n), shape(1, n, n)),
        in_specs=[smem] + [vmem] * 4,
        out_specs=(vmem, vmem),
        scratch_shapes=[pltpu.VMEM((1, 2, BOARD, LANES), jnp.float32)],
        compiler_params=params,
    )(role.reshape(1), state, info, far_state, far_info)
    home = []
    for i in range(devices):
        above = i >= half
        spot = 2 * ((i - half if above else i) // 2) + (1 if above else 0)
        home.append((i, spot + half if i % 2 else spot))
    return lax.ppermute(mean, "tm", home), lax.ppermute(cov, "tm", home)


def solution(mesh):
    return jax.shard_map(
        shards,
        mesh=mesh,
        in_specs=(P("tm", None), P("tm", None), P(), P(), P(), P(), P()),
        out_specs=(P("tm", None), P("tm", None, None)),
        check_vma=False,
    )
```

```python
import functools

import jax
import jax.numpy as jnp
from jax import lax
from jax.experimental import pallas as pl
from jax.experimental.pallas import tpu as pltpu
from jax.sharding import PartitionSpec as P

ROWS = 8
LANES = 128
VECTOR = 16
EXTRA = ROWS + ROWS // 2
BOARD = ROWS * (EXTRA + ROWS)
FAN = 4


def pieces(x, count):
    out = []
    for _ in range(count):
        out.append(x.astype(jnp.bfloat16))
        x = x - out[-1].astype(jnp.float32)
    return out


def left_of(x):
    high, low = pieces(x, 2)
    return jnp.concatenate([high, low, high], axis=1)


def right_of(x):
    high, low = pieces(x, 2)
    return jnp.concatenate([high, high, low], axis=1)


def left_moving(x):
    high, low = pieces(x, 2)
    return jnp.concatenate([high, low, high, high], axis=1)


def right_moving(x):
    high, low = pieces(x, 2)
    return jnp.concatenate([high, high, high, low], axis=0)


def join_nn(left, right):
    return lax.dot_general(
        left, right, (((1,), (0,)), ((), ())), preferred_element_type=jnp.float32
    )


def join_nt(left, right):
    return lax.dot_general(
        left, right, (((1,), (1,)), ((), ())), preferred_element_type=jnp.float32
    )


def spread_lane(x, lane):
    return jnp.broadcast_to(x[:, lane : lane + 1], x.shape)


def exact_nt(left, right):
    a, b, c = pieces(left, 3)
    p, q, r = pieces(right, 3)
    return join_nt(
        jnp.concatenate([a, a, b, a, b, c], axis=1), jnp.concatenate([p, q, p, r, q, p], axis=1)
    )


def exact_nn(left, right):
    a, b, c = pieces(left, 3)
    p, q, r = pieces(right, 3)
    return join_nn(
        jnp.concatenate([a, a, b, a, b, c], axis=1), jnp.concatenate([p, q, p, r, q, p], axis=0)
    )


def near_nn(left, right):
    high, low = pieces(right, 2)
    return join_nn(left_of(left), jnp.concatenate([high, high, low], axis=0))


def near_nt(left, right):
    return join_nt(left_of(left), right_of(right))


def factor_small(matrices, board, beside=()):
    beside = list(beside)
    done = 0
    side = matrices[0].shape[0]
    count = side // ROWS
    shape = (ROWS, side)
    row = lax.broadcasted_iota(jnp.int32, shape, 0)
    lane = lax.broadcasted_iota(jnp.int32, shape, 1)
    tasks = [[m[ROWS * k : ROWS * (k + 1)] for k in range(count)] for m in matrices]
    outs = [([], []) for m in matrices]
    heads = [[spread_lane(X[0], i) for i in range(ROWS)] for X in tasks]
    for k in range(count):
        base = ROWS * k
        more = k + 1 < count
        for t, (X, out) in enumerate(zip(tasks, outs)):

            def put(slot, values):
                board[t, k % 2, ROWS * slot : ROWS * (slot + 1)] = values

            def spread(slot, r):
                at = ROWS * slot + r
                return jnp.broadcast_to(board[t, k % 2, at : at + 1], shape)

            cols = heads[t]
            for i in range(ROWS):
                put(i, cols[i])
            block = {(r, i): spread(i, r) for i in range(ROWS) for r in range(i, ROWS)}
            nexts = [spread_lane(X[k + 1], base + i) for i in range(ROWS)] if more else []
            heads[t] = [spread_lane(X[k + 1], base + ROWS + i) for i in range(ROWS)] if more else []
            pivots = jnp.ones(shape, jnp.float32)
            for i in range(0, ROWS, 2):
                p = base + i
                while done < len(beside) and done * side <= p * len(beside):
                    beside[done]()
                    done += 1
                pair = (lane == p) | (lane == p + 1)
                a, b, c = block[i, i], block[i + 1, i], block[i + 1, i + 1]
                det = a * c - b * b
                ra = pltpu.reciprocal(a, approx=True)
                rdet = pltpu.reciprocal(det, approx=True)
                ratio = b * ra
                rest = range(i + 2, ROWS)
                firsts = {q: block[q, i] for q in rest}
                mixed = {q: a * block[q, i + 1] - b * firsts[q] for q in rest}
                seconds = {q: mixed[q] * ra for q in rest}
                for q in rest:
                    for r in range(q, ROWS):
                        block[r, q] = (
                            block[r, q] - (firsts[r] * ra) * firsts[q] - (mixed[r] * rdet) * seconds[q]
                        )
                pivots = jnp.where(row == i, a, pivots)
                pivots = jnp.where(row == i + 1, det * ra, pivots)
                put(ROWS + i // 2, X[k])
                xp = spread(ROWS + i // 2, i)
                xp = jnp.where(lane == p, 1.0, jnp.where(lane == p + 1, 0.0, xp))
                xq = spread(ROWS + i // 2, i + 1)
                xq = jnp.where(lane == p + 1, 1.0, jnp.where(lane == p, 0.0, xq))
                xq = xq - ratio * xp
                xp_scaled = xp * ra
                xq_scaled = xq * (a * rdet)
                Z = jnp.where((row == i) & (lane == p), 1.0, X[k])
                if i + 2 < ROWS:
                    f0 = cols[i] * ra
                    f1 = (a * cols[i + 1] - b * cols[i]) * rdet
                    for q in rest:
                        cols[q] = cols[q] - f0 * firsts[q] - f1 * seconds[q]
                    m0 = jnp.where(row > i + 1, f0, 0.0)
                    m1 = jnp.where(row > i + 1, f1, 0.0)
                    Z = jnp.where((row > i + 1) & pair, 0.0, Z) - m0 * xp - m1 * xq
                X[k] = jnp.where(row == i + 1, xq, Z)
                if more:
                    g0, g1 = nexts[i], nexts[i + 1]
                    h0 = g0 * ra
                    g1 = a * g1 - b * g0
                    h1 = g1 * rdet
                    put(EXTRA + i, g0)
                    put(EXTRA + i + 1, g1 * ra)
                    for q in range(ROWS):
                        first, second = spread(EXTRA + i, q), spread(EXTRA + i + 1, q)
                        heads[t][q] = heads[t][q] - h0 * first - h1 * second
                    for q in rest:
                        nexts[q] = nexts[q] - h0 * firsts[q] - h1 * seconds[q]
                    X[k + 1] = jnp.where(pair, 0.0, X[k + 1]) - h0 * xp - h1 * xq
                for j in range(k + 2, count):
                    g0 = spread_lane(X[j], p)
                    g1 = spread_lane(X[j], p + 1) - ratio * g0
                    X[j] = jnp.where(pair, 0.0, X[j]) - g0 * xp_scaled - g1 * xq_scaled
            s = lax.rsqrt(pivots)
            s = s * (1.5 - 0.5 * pivots * s * s)
            scaled = X[k] * s
            diagonal = jnp.where(lane == row + base, pivots * s, 0.0)
            out[0].append(jnp.where(lane > row + base, scaled, diagonal))
            out[1].append(jnp.where(lane <= row + base, scaled, 0.0))
    return [(jnp.concatenate(u, axis=0), jnp.concatenate(v, axis=0)) for u, v in outs]


def factor(matrices, board):
    blocks = matrices[0].shape[0] // LANES
    if blocks == 1:
        return factor_small(matrices, board)

    def cut(m, i, j):
        return m[LANES * i : LANES * (i + 1), LANES * j : LANES * (j + 1)]

    zero = jnp.zeros((LANES, LANES), jnp.float32)
    uppers = [{} for m in matrices]
    lowers = [{} for m in matrices]
    inverses = [{} for m in matrices]
    for j in range(blocks):
        heads = []
        for m, U, L in zip(matrices, uppers, lowers):
            head = cut(m, j, j)
            for k in range(j):
                head = head - exact_nt(L[j, k], L[j, k])
            heads.append(head)
        for m, U, L, V, (u, v) in zip(
            matrices, uppers, lowers, inverses, factor_small(heads, board)
        ):
            U[j, j] = u
            V[j, j] = v
            for i in range(j + 1, blocks):
                right = cut(m, j, i)
                down = cut(m, i, j)
                for k in range(j):
                    right = right - exact_nn(L[j, k], U[k, i])
                    down = down - exact_nn(L[i, k], U[k, j])
                U[j, i] = exact_nn(v, right)
                L[i, j] = exact_nt(down, v)
    outs = []
    for U, L, V in zip(uppers, lowers, inverses):
        for i in range(blocks):
            for j in range(i):
                total = exact_nn(L[i, j], V[j, j])
                for k in range(j + 1, i):
                    total = total + exact_nn(L[i, k], V[k, j])
                V[i, j] = -exact_nn(V[i, i], total)
        whole = [
            jnp.concatenate(
                [
                    jnp.concatenate([D.get((i, j), zero) for j in range(blocks)], axis=1)
                    for i in range(blocks)
                ],
                axis=0,
            )
            for D in (U, V)
        ]
        outs.append(tuple(whole))
    return outs


def unit(side):
    row = lax.broadcasted_iota(jnp.int32, (side, side), 0)
    col = lax.broadcasted_iota(jnp.int32, (side, side), 1)
    return jnp.where(row == col, 1.0, 0.0)


def first_of(values):
    row = lax.broadcasted_iota(jnp.int32, (VECTOR, values.shape[1]), 0)
    return jnp.where(row == 0, values, 0.0)


def maps_kernel(
    transition_ref,
    sensing_ref,
    noise_ref,
    prior_ref,
    left_ref,
    right_ref,
    fresh_ref,
    sensed_noise_ref,
    sensed_fresh_ref,
):
    n = transition_ref.shape[0]
    o = sensing_ref.shape[0]
    transition = transition_ref[...]
    sensing = sensing_ref[...]
    noise = noise_ref[...]
    sensed = exact_nn(sensing, transition)
    maps = jnp.concatenate([transition, sensing, sensed], axis=0)
    high, low, least = pieces(maps, 3)
    right_ref[...] = jnp.concatenate([high, high, low, least], axis=1)
    left = jnp.concatenate([high, low, least, high], axis=1)
    left_ref[0:n] = left[0:n]
    left_ref[n:] = left[n + o :]
    sensed_noise_ref[...] = exact_nn(sensing, exact_nt(noise, sensing))
    carried = exact_nt(prior_ref[...], jnp.concatenate([transition, sensed], axis=0))
    fresh_ref[...] = exact_nn(transition, carried[:, 0:n]) + noise
    sensed_fresh_ref[...] = exact_nn(sensed, carried[:, n:])


def window_kernel(
    steps,
    times,
    begin_ref,
    rows_ref,
    left_ref,
    right_ref,
    noise_ref,
    fresh_ref,
    sensed_noise_ref,
    sensed_fresh_ref,
    mean_ref,
    state_ref,
    info_ref,
    spread_ref,
    before_ref,
    moved_ref,
    waiting_ref,
    inverse_ref,
    sensed_ref,
    board,
):
    n = noise_ref.shape[0]
    o = sensed_noise_ref.shape[0]
    begin = begin_ref[0]
    eye_sense = unit(o)

    def wrap(t):
        return jnp.where(t >= times, t - times, t)

    def line_at(k):
        return rows_ref[pl.ds(jnp.minimum(k, steps - 1), 1), :]

    def innovation(k, spread):
        return spread + sensed_noise_ref[...] + eye_sense * line_at(k)[:, o:]

    moved_ref[0:n] = unit(n)
    moved_ref[n:] = jnp.zeros((VECTOR, n), jnp.float32)
    waiting_ref[...] = jnp.zeros_like(waiting_ref)
    inverse_ref[...] = jnp.zeros_like(inverse_ref)
    info_ref[...] = jnp.zeros_like(info_ref)
    spread_ref[...] = jnp.where(begin == 0, fresh_ref[...], noise_ref[...])
    sensed_ref[...] = innovation(0, jnp.where(begin == 0, sensed_fresh_ref[...], 0.0))

    def update():
        white = join_nt(waiting_ref[...], inverse_ref[...])
        left = left_of(white[n:])
        info_ref[...] = info_ref[...] + join_nt(left, right_of(white[n : 2 * n]))
        return moved_ref[...] - join_nt(left, right_of(white[0:n])), white[0:n]

    def step(k, carry):
        now = wrap(begin + k)
        renewed = wrap(now + 1) == 0
        cuts = [(lo, min(n, lo + LANES)) for lo in range(0, n, LANES)]
        tall = [(lo, hi + (VECTOR if hi == n else 0)) for lo, hi in cuts]
        held = {}

        def see(lo, hi):
            held["seen", lo] = join_nt(left_moving(spread_ref[lo:hi]), right_ref[...])

        def prepare():
            held["seen"] = jnp.concatenate([held["seen", lo] for lo, _ in cuts], axis=0)
            held["ready"] = right_moving(held["seen"])

        def look_ahead(lo, hi):
            held["ahead", lo] = join_nn(left_ref[lo:hi], held["ready"][:, 0 : n + o])

        def sense_ahead():
            held["sensed"] = join_nn(left_ref[n:], held["ready"][:, n:])

        def whiten_gain():
            gain = join_nt(waiting_ref[0:n], inverse_ref[...])
            held["gain"] = right_of(gain)

        def whiten_move():
            white = join_nt(waiting_ref[n:], inverse_ref[...])
            held["left"] = left_of(white)
            held["right"] = right_of(white[0:n])

        def inform(lo, hi):
            change = join_nt(held["left"][lo:hi], held["right"])
            info_ref[lo:hi] = info_ref[lo:hi] + change

        def correct(lo, hi):
            move = moved_ref[lo:hi] - join_nt(held["left"][lo:hi], held["gain"])
            start = jnp.zeros((min(hi, n) - lo, n), jnp.float32)
            if hi > n:
                start = jnp.concatenate([start, first_of(mean_ref[...])], axis=0)
            held["move", lo] = left_moving(jnp.where(now == 0, start, move))

        def advance(lo, hi):
            moved_ref[lo:hi] = join_nt(held["move", lo], right_ref[0:n])

        def err(lo, hi):
            errors = join_nt(held["move", lo], right_ref[n + o :])
            if hi > n:
                line = first_of(line_at(k)[:, 0:o])
                errors = jnp.concatenate([errors[: n - lo], errors[n - lo :] - line], axis=0)
            waiting_ref[n + lo : n + hi] = left_of(errors)

        def keep():
            waiting_ref[0:n] = left_of(held["seen"][:, n : n + o])
            before_ref[...] = spread_ref[...]

        beside = [functools.partial(see, *cut) for cut in cuts]
        beside += [whiten_gain, prepare, whiten_move]
        beside += [functools.partial(look_ahead, *cut) for cut in cuts]
        beside += [sense_ahead]
        beside += [functools.partial(correct, *cut) for cut in tall]
        beside += [functools.partial(inform, *cut) for cut in tall]
        beside += [functools.partial(advance, *cut) for cut in tall]
        beside += [functools.partial(err, *cut) for cut in tall]
        beside += [keep]
        ((_, inverse),) = factor_small([sensed_ref[...]], board, beside)
        ahead = jnp.concatenate([held["ahead", lo] for lo, _ in cuts], axis=0)
        gained = exact_nt(held["sensed"][:, 0:o], inverse)
        sensed = held["sensed"][:, o:] - exact_nt(gained, gained)
        sensed_ref[...] = innovation(k + 1, jnp.where(renewed, sensed_fresh_ref[...], sensed))
        inverse_right = right_of(inverse)
        inverse_ref[...] = inverse_right
        gain = join_nt(left_of(ahead[:, n:]), inverse_right)
        later = ahead[:, 0:n] + noise_ref[...] - join_nt(left_of(gain), right_of(gain))
        spread_ref[...] = jnp.where(renewed, fresh_ref[...], later)
        return carry

    lax.fori_loop(0, steps, step, 0)
    move, gain = update()
    ((root, _),) = factor([before_ref[...] - near_nt(gain, gain)], board)
    state_ref[0:n] = root
    state_ref[n:] = move


def meet_kernel(
    role_ref, state_ref, info_ref, far_state_ref, far_info_ref, mean_ref, cov_ref, board
):
    n = state_ref.shape[1]
    late = role_ref[0] == 1
    eye = unit(n)

    def of_cut(rows, near, far):
        return jnp.where(late, far[rows], near[rows])

    def of_middle(rows, near, far):
        return jnp.where(late, near[rows], far[rows])

    root_rows, move_rows, center_rows = slice(0, n), slice(n, 2 * n), slice(2 * n, 2 * n + VECTOR)
    info_rows, vector_rows = slice(0, n), slice(n, n + VECTOR)
    cut_root = of_cut(root_rows, state_ref, far_state_ref)
    cut_center = of_cut(center_rows, state_ref, far_state_ref)
    cut_info = of_cut(info_rows, info_ref, far_info_ref)
    cut_vector = of_cut(vector_rows, info_ref, far_info_ref)
    mid_root = of_middle(root_rows, state_ref, far_state_ref)
    move = of_middle(move_rows, state_ref, far_state_ref)
    mid_center = of_middle(center_rows, state_ref, far_state_ref)
    mid_info = of_middle(info_rows, info_ref, far_info_ref)
    mid_vector = of_middle(vector_rows, info_ref, far_info_ref)

    rooted = exact_nt(cut_info, mid_root)
    ((_, inner),) = factor([eye + exact_nn(mid_root, rooted)], board)
    carried = near_nn(inner, mid_root)
    mixing = near_nt(rooted, inner)
    kept = cut_info - near_nt(mixing, mixing)
    early_info = mid_info + near_nt(near_nn(move, kept), move)
    ((_, last),) = factor(
        [eye + exact_nn(cut_root, exact_nt(early_info, cut_root))], board
    )
    residue = -cut_vector - near_nn(mid_center, cut_info)
    residue_carried = near_nt(residue, carried)
    early_vector = near_nt(residue - near_nt(residue_carried, mixing), move) - mid_vector
    pull = early_vector - near_nn(cut_center, early_info)
    cut_root_t = cut_root.T
    through = move - near_nn(near_nn(move, mixing), carried)
    through_center = mid_center + near_nn(residue_carried, carried)
    carried_t = carried.T
    leftover = near_nt(carried_t, carried_t)
    late_root = near_nt(through.T, cut_root)
    early_root = near_nt(cut_root_t, last)
    early_center = cut_center + near_nt(near_nn(pull, early_root), early_root)
    root = near_nt(jnp.where(late, late_root, cut_root_t), last)
    cov_ref[0] = jnp.where(late, leftover, 0.0) + near_nt(root, root)
    late_center = near_nn(early_center, through) + through_center
    mean_ref[...] = jnp.where(late, late_center, early_center)[0:1]


def begin_of(device, devices):
    quarter = devices // 4
    chip = device // 2
    upper = chip // quarter
    split = 2 * (chip - quarter * upper) + upper
    role = device % 2
    return (split + 1 + (1 - role) * (devices - devices // 2)) % devices


def gather_rows(rows, steps, axis):
    devices = lax.axis_size(axis)
    begins = [begin_of(i, devices) for i in range(devices)]
    holder = {begin: i for i, begin in enumerate(begins)}
    held = min(FAN, steps)
    parts = [
        lax.ppermute(rows, axis, [((begins[i] + j) % devices, i) for i in range(devices)])
        for j in range(held)
    ]
    rows = jnp.concatenate(parts, axis=0)
    while held < steps:
        parts = [rows]
        for m in range(1, FAN):
            size = min(held, steps - m * held)
            if size > 0:
                pairs = [(holder[(begins[i] + m * held) % devices], i) for i in range(devices)]
                parts.append(lax.ppermute(rows[:size], axis, pairs))
        rows = jnp.concatenate(parts, axis=0)
        held = min(steps, FAN * held)
    return rows


def shards(
    measurements, noise_levels, transition, sensing, process_noise, prior_mean, prior_covariance
):
    n = transition.shape[0]
    o = sensing.shape[0]
    devices = lax.axis_size("tm")
    half = devices // 2
    device = lax.axis_index("tm").astype(jnp.int32)
    role = device % 2
    begin = begin_of(device, devices)

    rows = gather_rows(jnp.concatenate([measurements, noise_levels], axis=1), half, "tm")
    vmem = pl.BlockSpec(memory_space=pltpu.VMEM)
    smem = pl.BlockSpec(memory_space=pltpu.SMEM)
    params = pltpu.CompilerParams(vmem_limit_bytes=48 * 1024 * 1024)

    def shape(*dims):
        return jax.ShapeDtypeStruct(dims, jnp.float32)

    left, right, fresh, sensed_noise, sensed_fresh = pl.pallas_call(
        maps_kernel,
        out_shape=(
            jax.ShapeDtypeStruct((n + o, 4 * n), jnp.bfloat16),
            jax.ShapeDtypeStruct((n + 2 * o, 4 * n), jnp.bfloat16),
            shape(n, n),
            shape(o, o),
            shape(o, o),
        ),
        in_specs=[vmem] * 4,
        out_specs=(vmem,) * 5,
        compiler_params=params,
    )(transition, sensing, process_noise, prior_covariance)
    state, info = pl.pallas_call(
        functools.partial(window_kernel, half, devices),
        out_shape=(shape(2 * n + VECTOR, n), shape(n + VECTOR, n)),
        in_specs=[smem] + [vmem] * 8,
        out_specs=(vmem, vmem),
        scratch_shapes=[
            pltpu.VMEM((n, n), jnp.float32),
            pltpu.VMEM((n, n), jnp.float32),
            pltpu.VMEM((n + VECTOR, n), jnp.float32),
            pltpu.VMEM((2 * n + VECTOR, 3 * o), jnp.bfloat16),
            pltpu.VMEM((o, 3 * o), jnp.bfloat16),
            pltpu.VMEM((o, o), jnp.float32),
            pltpu.VMEM((1, 2, BOARD, o), jnp.float32),
        ],
        compiler_params=params,
    )(
        begin.reshape(1),
        rows,
        left,
        right,
        process_noise,
        fresh,
        sensed_noise,
        sensed_fresh,
        prior_mean.reshape(1, n),
    )
    swap = [(i, i ^ 1) for i in range(devices)]
    far_state = lax.ppermute(state, "tm", swap)
    far_info = lax.ppermute(info, "tm", swap)
    mean, cov = pl.pallas_call(
        meet_kernel,
        out_shape=(shape(1, n), shape(1, n, n)),
        in_specs=[smem] + [vmem] * 4,
        out_specs=(vmem, vmem),
        scratch_shapes=[pltpu.VMEM((1, 2, BOARD, LANES), jnp.float32)],
        compiler_params=params,
    )(role.reshape(1), state, info, far_state, far_info)
    home = []
    for i in range(devices):
        above = i >= half
        spot = 2 * ((i - half if above else i) // 2) + (1 if above else 0)
        home.append((i, spot + half if i % 2 else spot))
    return lax.ppermute(mean, "tm", home), lax.ppermute(cov, "tm", home)


def solution(mesh):
    return jax.shard_map(
        shards,
        mesh=mesh,
        in_specs=(P("tm", None), P("tm", None), P(), P(), P(), P(), P()),
        out_specs=(P("tm", None), P("tm", None, None)),
        check_vma=False,
    )
```

```python
import functools

import jax
import jax.numpy as jnp
from jax import lax
from jax.experimental import pallas as pl
from jax.experimental.pallas import tpu as pltpu
from jax.sharding import PartitionSpec as P

ROWS = 8
LANES = 128
VECTOR = 16
GROUP = 8
LEAD = 2
EXTRA = ROWS + ROWS // 2
BOARD = ROWS * (EXTRA + ROWS)
FAN = 4
DIRECT = 4


def dot_nn(left, right):
    return lax.dot_general(
        left,
        right,
        (((1,), (0,)), ((), ())),
        precision=lax.Precision.HIGHEST,
        preferred_element_type=jnp.float32,
    )


def dot_nt(left, right):
    return lax.dot_general(
        left,
        right,
        (((1,), (1,)), ((), ())),
        precision=lax.Precision.HIGHEST,
        preferred_element_type=jnp.float32,
    )


def pieces(x, count):
    out = []
    for _ in range(count):
        out.append(x.astype(jnp.bfloat16))
        x = x - out[-1].astype(jnp.float32)
    return out


def left_of(x):
    high, low = pieces(x, 2)
    return jnp.concatenate([high, low, high], axis=1)


def right_of(x):
    high, low = pieces(x, 2)
    return jnp.concatenate([high, high, low], axis=1)


def left_moving(x):
    high, low = pieces(x, 2)
    return jnp.concatenate([high, low, high, high], axis=1)


def right_moving(x):
    high, low = pieces(x, 2)
    return jnp.concatenate([high, high, high, low], axis=0)


def join_nn(left, right):
    return lax.dot_general(
        left, right, (((1,), (0,)), ((), ())), preferred_element_type=jnp.float32
    )


def join_nt(left, right):
    return lax.dot_general(
        left, right, (((1,), (1,)), ((), ())), preferred_element_type=jnp.float32
    )


def spread_lane(x, lane):
    return jnp.broadcast_to(x[:, lane : lane + 1], x.shape)


def exact_tn(left, right):
    a, b, c = pieces(left, 3)
    p, q, r = pieces(right, 3)
    return lax.dot_general(
        jnp.concatenate([a, a, b, a, b, c], axis=0),
        jnp.concatenate([p, q, p, r, q, p], axis=0),
        (((0,), (0,)), ((), ())),
        preferred_element_type=jnp.float32,
    )


def exact_nt(left, right):
    a, b, c = pieces(left, 3)
    p, q, r = pieces(right, 3)
    return join_nt(
        jnp.concatenate([a, a, b, a, b, c], axis=1), jnp.concatenate([p, q, p, r, q, p], axis=1)
    )


def exact_nn(left, right):
    a, b, c = pieces(left, 3)
    p, q, r = pieces(right, 3)
    return join_nn(
        jnp.concatenate([a, a, b, a, b, c], axis=1), jnp.concatenate([p, q, p, r, q, p], axis=0)
    )


def near_nn(left, right):
    high, low = pieces(right, 2)
    return join_nn(left_of(left), jnp.concatenate([high, high, low], axis=0))


def near_nt(left, right):
    return join_nt(left_of(left), right_of(right))


def factor_small(matrices, board, group=None):
    side = matrices[0].shape[0]
    count = side // ROWS
    group = group or count
    shape = (ROWS, side)
    row = lax.broadcasted_iota(jnp.int32, shape, 0)
    lane = lax.broadcasted_iota(jnp.int32, shape, 1)
    tasks = [[m[ROWS * k : ROWS * (k + 1)] for k in range(count)] for m in matrices]
    outs = [([], []) for m in matrices]
    heads = [[spread_lane(X[0], i) for i in range(ROWS)] for X in tasks]
    for k in range(count):
        base = ROWS * k
        more = k + 1 < count
        stop = min(count, (k // group + 1) * group)
        reach = min(count, stop + LEAD)
        for t, (X, out) in enumerate(zip(tasks, outs)):

            def put(slot, values):
                board[t, k % 2, ROWS * slot : ROWS * (slot + 1)] = values

            def spread(slot, r):
                at = ROWS * slot + r
                return jnp.broadcast_to(board[t, k % 2, at : at + 1], shape)

            cols = heads[t]
            for i in range(ROWS):
                put(i, cols[i])
            block = {(r, i): spread(i, r) for i in range(ROWS) for r in range(i, ROWS)}
            nexts = [spread_lane(X[k + 1], base + i) for i in range(ROWS)] if more else []
            heads[t] = [spread_lane(X[k + 1], base + ROWS + i) for i in range(ROWS)] if more else []
            pivots = jnp.ones(shape, jnp.float32)
            for i in range(0, ROWS, 2):
                p = base + i
                pair = (lane == p) | (lane == p + 1)
                a, b, c = block[i, i], block[i + 1, i], block[i + 1, i + 1]
                det = a * c - b * b
                ra = pltpu.reciprocal(a, approx=True)
                rdet = pltpu.reciprocal(det, approx=True)
                ratio = b * ra
                rest = range(i + 2, ROWS)
                firsts = {q: block[q, i] for q in rest}
                mixed = {q: a * block[q, i + 1] - b * firsts[q] for q in rest}
                seconds = {q: mixed[q] * ra for q in rest}
                for q in rest:
                    for r in range(q, ROWS):
                        block[r, q] = (
                            block[r, q] - (firsts[r] * ra) * firsts[q] - (mixed[r] * rdet) * seconds[q]
                        )
                pivots = jnp.where(row == i, a, pivots)
                pivots = jnp.where(row == i + 1, det * ra, pivots)
                put(ROWS + i // 2, X[k])
                xp = spread(ROWS + i // 2, i)
                xp = jnp.where(lane == p, 1.0, jnp.where(lane == p + 1, 0.0, xp))
                xq = spread(ROWS + i // 2, i + 1)
                xq = jnp.where(lane == p + 1, 1.0, jnp.where(lane == p, 0.0, xq))
                xq = xq - ratio * xp
                xp_scaled = xp * ra
                xq_scaled = xq * (a * rdet)
                Z = jnp.where((row == i) & (lane == p), 1.0, X[k])
                if i + 2 < ROWS:
                    f0 = cols[i] * ra
                    f1 = (a * cols[i + 1] - b * cols[i]) * rdet
                    for q in rest:
                        cols[q] = cols[q] - f0 * firsts[q] - f1 * seconds[q]
                    m0 = jnp.where(row > i + 1, f0, 0.0)
                    m1 = jnp.where(row > i + 1, f1, 0.0)
                    Z = jnp.where((row > i + 1) & pair, 0.0, Z) - m0 * xp - m1 * xq
                X[k] = jnp.where(row == i + 1, xq, Z)
                if more:
                    g0, g1 = nexts[i], nexts[i + 1]
                    h0 = g0 * ra
                    g1 = a * g1 - b * g0
                    h1 = g1 * rdet
                    put(EXTRA + i, g0)
                    put(EXTRA + i + 1, g1 * ra)
                    for q in range(ROWS):
                        first, second = spread(EXTRA + i, q), spread(EXTRA + i + 1, q)
                        heads[t][q] = heads[t][q] - h0 * first - h1 * second
                    for q in rest:
                        nexts[q] = nexts[q] - h0 * firsts[q] - h1 * seconds[q]
                    X[k + 1] = jnp.where(pair, 0.0, X[k + 1]) - h0 * xp - h1 * xq
                for j in range(k + 2, reach):
                    g0 = spread_lane(X[j], p)
                    g1 = spread_lane(X[j], p + 1) - ratio * g0
                    X[j] = jnp.where(pair, 0.0, X[j]) - g0 * xp_scaled - g1 * xq_scaled
            s = lax.rsqrt(pivots)
            s = s * (1.5 - 0.5 * pivots * s * s)
            scaled = X[k] * s
            diagonal = jnp.where(lane == row + base, pivots * s, 0.0)
            out[0].append(jnp.where(lane > row + base, scaled, diagonal))
            out[1].append(jnp.where(lane <= row + base, scaled, 0.0))
            if k + 1 == stop and reach < count:
                begin = stop - group
                low, high = ROWS * begin, ROWS * stop
                uppers = jnp.concatenate(out[0][begin:stop], axis=0)
                lowers = jnp.concatenate(out[1][begin:stop], axis=0)
                after = lax.broadcasted_iota(jnp.int32, uppers.shape, 1) >= high
                change = exact_tn(uppers, jnp.where(after, uppers, lowers))
                here = (lane >= low) & (lane < high)
                for j in range(reach, count):
                    X[j] = jnp.where(here, 0.0, X[j]) - change[ROWS * j : ROWS * (j + 1)]
    return [(jnp.concatenate(u, axis=0), jnp.concatenate(v, axis=0)) for u, v in outs]


def factor(matrices, board):
    blocks = matrices[0].shape[0] // LANES
    if blocks == 1:
        return factor_small(matrices, board, GROUP)

    def cut(m, i, j):
        return m[LANES * i : LANES * (i + 1), LANES * j : LANES * (j + 1)]

    zero = jnp.zeros((LANES, LANES), jnp.float32)
    uppers = [{} for m in matrices]
    lowers = [{} for m in matrices]
    inverses = [{} for m in matrices]
    for j in range(blocks):
        heads = []
        for m, U, L in zip(matrices, uppers, lowers):
            head = cut(m, j, j)
            for k in range(j):
                head = head - exact_nt(L[j, k], L[j, k])
            heads.append(head)
        for m, U, L, V, (u, v) in zip(
            matrices, uppers, lowers, inverses, factor_small(heads, board, GROUP)
        ):
            U[j, j] = u
            V[j, j] = v
            for i in range(j + 1, blocks):
                right = cut(m, j, i)
                down = cut(m, i, j)
                for k in range(j):
                    right = right - exact_nn(L[j, k], U[k, i])
                    down = down - exact_nn(L[i, k], U[k, j])
                U[j, i] = exact_nn(v, right)
                L[i, j] = exact_nt(down, v)
    outs = []
    for U, L, V in zip(uppers, lowers, inverses):
        for i in range(blocks):
            for j in range(i):
                total = exact_nn(L[i, j], V[j, j])
                for k in range(j + 1, i):
                    total = total + exact_nn(L[i, k], V[k, j])
                V[i, j] = -exact_nn(V[i, i], total)
        whole = [
            jnp.concatenate(
                [
                    jnp.concatenate([D.get((i, j), zero) for j in range(blocks)], axis=1)
                    for i in range(blocks)
                ],
                axis=0,
            )
            for D in (U, V)
        ]
        outs.append(tuple(whole))
    return outs


def unit(side):
    row = lax.broadcasted_iota(jnp.int32, (side, side), 0)
    col = lax.broadcasted_iota(jnp.int32, (side, side), 1)
    return jnp.where(row == col, 1.0, 0.0)


def first_of(values):
    row = lax.broadcasted_iota(jnp.int32, (VECTOR, values.shape[1]), 0)
    return jnp.where(row == 0, values, 0.0)


def maps_kernel(transition_ref, sensing_ref, noise_ref, left_ref, right_ref, consts_ref):
    n = transition_ref.shape[0]
    transition = transition_ref[...]
    sensing = sensing_ref[...]
    noise = noise_ref[...]
    maps = jnp.concatenate([transition, dot_nn(sensing, transition)], axis=0)
    high, low, least = pieces(maps, 3)
    left_ref[...] = jnp.concatenate([high, low, least, high], axis=1)
    right_ref[...] = jnp.concatenate([high, high, low, least], axis=1)
    noise_sensed = dot_nt(noise, sensing)
    consts_ref[0:n, 0:n] = noise
    consts_ref[0:n, n:] = noise_sensed
    consts_ref[n:, 0:n] = jnp.zeros((sensing.shape[0], n), jnp.float32)
    consts_ref[n:, n:] = dot_nn(sensing, noise_sensed)


def window_kernel(
    steps,
    times,
    begin_ref,
    rows_ref,
    left_ref,
    right_ref,
    consts_ref,
    mean_ref,
    prior_ref,
    state_ref,
    info_ref,
    moved_ref,
    waiting_ref,
    inverse_ref,
    sensed_ref,
    board,
):
    n = prior_ref.shape[0]
    o = left_ref.shape[0] - n
    begin = begin_ref[0]
    eye_sense = unit(o)

    def wrap(t):
        return jnp.where(t >= times, t - times, t)

    def line_at(k):
        return rows_ref[pl.ds(jnp.minimum(k, steps - 1), 1), :]

    def first_spread(k, spread):
        line = line_at(k)
        return spread + consts_ref[n:, n:] + eye_sense * line[:, o:]

    moved_ref[0:n] = jnp.zeros((n, n), jnp.float32)
    moved_ref[n : 2 * n] = unit(n)
    moved_ref[2 * n :] = jnp.zeros((VECTOR, n), jnp.float32)
    waiting_ref[...] = jnp.zeros_like(waiting_ref)
    inverse_ref[...] = jnp.zeros_like(inverse_ref)
    info_ref[...] = jnp.zeros_like(info_ref)

    def through_sensed(spread):
        half = join_nt(left_moving(spread), right_ref[n:])
        return join_nn(left_ref[n:], right_moving(half))

    sensed_ref[...] = first_spread(
        0, jnp.where(begin == 0, through_sensed(prior_ref[...]), 0.0)
    )

    def update():
        white = join_nt(waiting_ref[...], inverse_ref[...])
        left = left_of(white)
        info_ref[...] = info_ref[...] + join_nt(left[n:], right_of(white[n : 2 * n]))
        return moved_ref[...] - join_nt(left, right_of(white[0:n]))

    def step(k, carry):
        ((_, inverse),) = factor_small([sensed_ref[...]], board)
        now = wrap(begin + k)
        later = wrap(now + 1)
        state = update()
        state = jnp.where(
            now == 0,
            jnp.concatenate(
                [prior_ref[...], jnp.zeros((n, n), jnp.float32), first_of(mean_ref[...])], axis=0
            ),
            state,
        )
        moved = join_nt(left_moving(state), right_ref[...])
        ahead = join_nn(left_ref[0:n], right_moving(moved[0:n])) + consts_ref[0:n]
        moved_ref[0:n] = ahead[:, 0:n]
        moved_ref[n:] = moved[n:, 0:n]
        waiting_ref[0:n] = left_of(ahead[:, n:])
        waiting_ref[n : 2 * n] = left_of(moved[n : 2 * n, n:])
        waiting_ref[2 * n :] = left_of(moved[2 * n :, n:] - first_of(line_at(k)[:, 0:o]))
        kept = through_sensed(jnp.where(later == 0, prior_ref[...], ahead[:, 0:n]))
        gained = exact_nt(join_nn(left_ref[n:], right_moving(ahead[:, n:])), inverse)
        gained = jnp.where(later == 0, 0.0, gained)
        sensed_ref[...] = first_spread(k + 1, kept - exact_nt(gained, gained))
        inverse_ref[...] = right_of(inverse)
        return carry

    lax.fori_loop(0, steps, step, 0)
    state = update()
    ((root, _),) = factor([state[0:n]], board)
    state_ref[0:n] = root
    state_ref[n:] = state[n:]


def meet_kernel(
    role_ref, state_ref, info_ref, far_state_ref, far_info_ref, packed_ref, board
):
    n = state_ref.shape[1]
    late = role_ref[0] == 1
    eye = unit(n)

    def of_cut(rows, near, far):
        return jnp.where(late, far[rows], near[rows])

    def of_middle(rows, near, far):
        return jnp.where(late, near[rows], far[rows])

    root_rows, move_rows, center_rows = slice(0, n), slice(n, 2 * n), slice(2 * n, 2 * n + VECTOR)
    info_rows, vector_rows = slice(0, n), slice(n, n + VECTOR)
    cut_root = of_cut(root_rows, state_ref, far_state_ref)
    cut_center = of_cut(center_rows, state_ref, far_state_ref)
    cut_info = of_cut(info_rows, info_ref, far_info_ref)
    cut_vector = of_cut(vector_rows, info_ref, far_info_ref)
    mid_root = of_middle(root_rows, state_ref, far_state_ref)
    move = of_middle(move_rows, state_ref, far_state_ref)
    mid_center = of_middle(center_rows, state_ref, far_state_ref)
    mid_info = of_middle(info_rows, info_ref, far_info_ref)
    mid_vector = of_middle(vector_rows, info_ref, far_info_ref)

    rooted = exact_nt(cut_info, mid_root)
    ((_, inner),) = factor([eye + exact_nn(mid_root, rooted)], board)
    carried = near_nn(inner, mid_root)
    mixing = near_nt(rooted, inner)
    kept = cut_info - near_nt(mixing, mixing)
    early_info = mid_info + near_nt(near_nn(move, kept), move)
    ((_, last),) = factor(
        [eye + exact_nn(cut_root, exact_nt(early_info, cut_root))], board
    )
    residue = -cut_vector - near_nn(mid_center, cut_info)
    residue_carried = near_nt(residue, carried)
    early_vector = near_nt(residue - near_nt(residue_carried, mixing), move) - mid_vector
    pull = early_vector - near_nn(cut_center, early_info)
    cut_root_t = cut_root.T
    through = move - near_nn(near_nn(move, mixing), carried)
    through_center = mid_center + near_nn(residue_carried, carried)
    carried_t = carried.T
    leftover = near_nt(carried_t, carried_t)
    late_root = near_nt(through.T, cut_root)
    early_root = near_nt(cut_root_t, last)
    early_center = cut_center + near_nt(near_nn(pull, early_root), early_root)
    root = near_nt(jnp.where(late, late_root, cut_root_t), last)
    cov = jnp.where(late, leftover, 0.0) + near_nt(root, root)
    late_center = near_nn(early_center, through) + through_center
    mean = jnp.where(late, late_center, early_center)[0:1]
    half = n // 2
    row, col = square(half)
    last_block = cov[half:, half:]
    diagonal = jnp.sum(jnp.where(row == col, last_block, 0.0), axis=0, keepdims=True)
    packed_ref[0:half, 0:half] = jnp.where(row >= col, cov[0:half, 0:half], last_block)
    packed_ref[0:half, half:] = cov[0:half, half:]
    line = lax.broadcasted_iota(jnp.int32, (ROWS, n), 0)
    diagonal = jnp.concatenate([diagonal, jnp.zeros_like(diagonal)], axis=1)
    packed_ref[half:] = jnp.where(line == 0, mean, jnp.where(line == 1, diagonal, 0.0))


def square(side):
    return (
        lax.broadcasted_iota(jnp.int32, (side, side), 0),
        lax.broadcasted_iota(jnp.int32, (side, side), 1),
    )


def unfold_kernel(packed_ref, mean_ref, cov_ref):
    half = packed_ref.shape[1] // 2
    row, col = square(half)
    both = packed_ref[0:half, 0:half]
    across = packed_ref[0:half, half:]
    above = jnp.where(row < col, both, 0.0)
    cov_ref[0, 0:half, 0:half] = jnp.where(row >= col, both, 0.0) + jnp.where(row > col, both, 0.0).T
    cov_ref[0, 0:half, half:] = across
    cov_ref[0, half:, 0:half] = across.T
    diagonal = jnp.where(row == col, packed_ref[half + 1 : half + 2, 0:half], 0.0)
    cov_ref[0, half:, half:] = above + above.T + diagonal
    mean_ref[...] = packed_ref[half : half + 1]


def begin_of(device, devices):
    quarter = devices // 4
    chip = device // 2
    upper = chip // quarter
    split = 2 * (chip - quarter * upper) + upper
    role = device % 2
    return (split + 1 + (1 - role) * (devices - devices // 2)) % devices


def gather_rows(rows, steps, axis):
    devices = lax.axis_size(axis)
    begins = [begin_of(i, devices) for i in range(devices)]
    holder = {begin: i for i, begin in enumerate(begins)}
    held = min(DIRECT, steps)
    parts = [
        lax.ppermute(rows, axis, [((begins[i] + j) % devices, i) for i in range(devices)])
        for j in range(held)
    ]
    rows = jnp.concatenate(parts, axis=0)
    while held < steps:
        parts = [rows]
        for m in range(1, FAN):
            size = min(held, steps - m * held)
            if size > 0:
                pairs = [(holder[(begins[i] + m * held) % devices], i) for i in range(devices)]
                parts.append(lax.ppermute(rows[:size], axis, pairs))
        rows = jnp.concatenate(parts, axis=0)
        held = min(steps, FAN * held)
    return rows


def shards(
    measurements, noise_levels, transition, sensing, process_noise, prior_mean, prior_covariance
):
    n = transition.shape[0]
    o = sensing.shape[0]
    devices = lax.axis_size("tm")
    half = devices // 2
    device = lax.axis_index("tm").astype(jnp.int32)
    role = device % 2
    begin = begin_of(device, devices)

    rows = gather_rows(jnp.concatenate([measurements, noise_levels], axis=1), half, "tm")
    vmem = pl.BlockSpec(memory_space=pltpu.VMEM)
    smem = pl.BlockSpec(memory_space=pltpu.SMEM)
    params = pltpu.CompilerParams(vmem_limit_bytes=48 * 1024 * 1024)

    def shape(*dims):
        return jax.ShapeDtypeStruct(dims, jnp.float32)

    passes = jax.ShapeDtypeStruct((n + o, 4 * n), jnp.bfloat16)
    left, right, consts = pl.pallas_call(
        maps_kernel,
        out_shape=(passes, passes, shape(n + o, n + o)),
        in_specs=[vmem] * 3,
        out_specs=(vmem, vmem, vmem),
        compiler_params=params,
    )(transition, sensing, process_noise)
    state, info = pl.pallas_call(
        functools.partial(window_kernel, half, devices),
        out_shape=(shape(2 * n + VECTOR, n), shape(n + VECTOR, n)),
        in_specs=[smem] + [vmem] * 6,
        out_specs=(vmem, vmem),
        scratch_shapes=[
            pltpu.VMEM((2 * n + VECTOR, n), jnp.float32),
            pltpu.VMEM((2 * n + VECTOR, 3 * o), jnp.bfloat16),
            pltpu.VMEM((o, 3 * o), jnp.bfloat16),
            pltpu.VMEM((o, o), jnp.float32),
            pltpu.VMEM((1, 2, BOARD, o), jnp.float32),
        ],
        compiler_params=params,
    )(begin.reshape(1), rows, left, right, consts, prior_mean.reshape(1, n), prior_covariance)
    swap = [(i, i ^ 1) for i in range(devices)]
    far_state = lax.ppermute(state, "tm", swap)
    far_info = lax.ppermute(info, "tm", swap)
    packed = pl.pallas_call(
        meet_kernel,
        out_shape=shape(n // 2 + ROWS, n),
        in_specs=[smem] + [vmem] * 4,
        out_specs=vmem,
        scratch_shapes=[pltpu.VMEM((1, 2, BOARD, LANES), jnp.float32)],
        compiler_params=params,
    )(role.reshape(1), state, info, far_state, far_info)
    home = []
    for i in range(devices):
        above = i >= half
        spot = 2 * ((i - half if above else i) // 2) + (1 if above else 0)
        home.append((i, spot + half if i % 2 else spot))
    return pl.pallas_call(
        unfold_kernel,
        out_shape=(shape(1, n), shape(1, n, n)),
        in_specs=[vmem],
        out_specs=(vmem, vmem),
        compiler_params=params,
    )(lax.ppermute(packed, "tm", home))


def solution(mesh):
    return jax.shard_map(
        shards,
        mesh=mesh,
        in_specs=(P("tm", None), P("tm", None), P(), P(), P(), P(), P()),
        out_specs=(P("tm", None), P("tm", None, None)),
        check_vma=False,
    )
```

```python
import functools

import jax
import jax.numpy as jnp
from jax import lax
from jax.experimental import pallas as pl
from jax.experimental.pallas import tpu as pltpu
from jax.sharding import PartitionSpec as P

ROWS = 8
LANES = 128
VECTOR = 16
GROUP = 8
LEAD = 2
EXTRA = ROWS + ROWS // 2
BOARD = ROWS * (EXTRA + ROWS)


def dot_nn(left, right):
    return lax.dot_general(
        left,
        right,
        (((1,), (0,)), ((), ())),
        precision=lax.Precision.HIGHEST,
        preferred_element_type=jnp.float32,
    )


def dot_nt(left, right):
    return lax.dot_general(
        left,
        right,
        (((1,), (1,)), ((), ())),
        precision=lax.Precision.HIGHEST,
        preferred_element_type=jnp.float32,
    )


def pieces(x, count):
    out = []
    for _ in range(count):
        out.append(x.astype(jnp.bfloat16))
        x = x - out[-1].astype(jnp.float32)
    return out


def left_of(x):
    high, low = pieces(x, 2)
    return jnp.concatenate([high, low, high], axis=1)


def right_of(x):
    high, low = pieces(x, 2)
    return jnp.concatenate([high, high, low], axis=1)


def left_moving(x):
    high, low = pieces(x, 2)
    return jnp.concatenate([high, low, high, high], axis=1)


def right_moving(x):
    high, low = pieces(x, 2)
    return jnp.concatenate([high, high, high, low], axis=0)


def join_nn(left, right):
    return lax.dot_general(
        left, right, (((1,), (0,)), ((), ())), preferred_element_type=jnp.float32
    )


def join_nt(left, right):
    return lax.dot_general(
        left, right, (((1,), (1,)), ((), ())), preferred_element_type=jnp.float32
    )


def spread_lane(x, lane):
    return jnp.broadcast_to(x[:, lane : lane + 1], x.shape)


def exact_tn(left, right):
    a, b, c = pieces(left, 3)
    p, q, r = pieces(right, 3)
    return lax.dot_general(
        jnp.concatenate([a, a, b, a, b, c], axis=0),
        jnp.concatenate([p, q, p, r, q, p], axis=0),
        (((0,), (0,)), ((), ())),
        preferred_element_type=jnp.float32,
    )


def exact_nt(left, right):
    a, b, c = pieces(left, 3)
    p, q, r = pieces(right, 3)
    return join_nt(
        jnp.concatenate([a, a, b, a, b, c], axis=1), jnp.concatenate([p, q, p, r, q, p], axis=1)
    )


def exact_nn(left, right):
    a, b, c = pieces(left, 3)
    p, q, r = pieces(right, 3)
    return join_nn(
        jnp.concatenate([a, a, b, a, b, c], axis=1), jnp.concatenate([p, q, p, r, q, p], axis=0)
    )


def near_nn(left, right):
    high, low = pieces(right, 2)
    return join_nn(left_of(left), jnp.concatenate([high, high, low], axis=0))


def near_nt(left, right):
    return join_nt(left_of(left), right_of(right))


def factor_small(matrices, board, group=None):
    side = matrices[0].shape[0]
    count = side // ROWS
    group = group or count
    shape = (ROWS, side)
    row = lax.broadcasted_iota(jnp.int32, shape, 0)
    lane = lax.broadcasted_iota(jnp.int32, shape, 1)
    tasks = [[m[ROWS * k : ROWS * (k + 1)] for k in range(count)] for m in matrices]
    outs = [([], []) for m in matrices]
    heads = [[spread_lane(X[0], i) for i in range(ROWS)] for X in tasks]
    for k in range(count):
        base = ROWS * k
        more = k + 1 < count
        stop = min(count, (k // group + 1) * group)
        reach = min(count, stop + LEAD)
        for t, (X, out) in enumerate(zip(tasks, outs)):

            def put(slot, values):
                board[t, k % 2, ROWS * slot : ROWS * (slot + 1)] = values

            def spread(slot, r):
                at = ROWS * slot + r
                return jnp.broadcast_to(board[t, k % 2, at : at + 1], shape)

            cols = heads[t]
            for i in range(ROWS):
                put(i, cols[i])
            block = {(r, i): spread(i, r) for i in range(ROWS) for r in range(i, ROWS)}
            nexts = [spread_lane(X[k + 1], base + i) for i in range(ROWS)] if more else []
            heads[t] = [spread_lane(X[k + 1], base + ROWS + i) for i in range(ROWS)] if more else []
            pivots = jnp.ones(shape, jnp.float32)
            for i in range(0, ROWS, 2):
                p = base + i
                pair = (lane == p) | (lane == p + 1)
                a, b, c = block[i, i], block[i + 1, i], block[i + 1, i + 1]
                det = a * c - b * b
                ra = pltpu.reciprocal(a, approx=True)
                rdet = pltpu.reciprocal(det, approx=True)
                ratio = b * ra
                rest = range(i + 2, ROWS)
                firsts = {q: block[q, i] for q in rest}
                mixed = {q: a * block[q, i + 1] - b * firsts[q] for q in rest}
                seconds = {q: mixed[q] * ra for q in rest}
                for q in rest:
                    for r in range(q, ROWS):
                        block[r, q] = (
                            block[r, q] - (firsts[r] * ra) * firsts[q] - (mixed[r] * rdet) * seconds[q]
                        )
                pivots = jnp.where(row == i, a, pivots)
                pivots = jnp.where(row == i + 1, det * ra, pivots)
                put(ROWS + i // 2, X[k])
                xp = spread(ROWS + i // 2, i)
                xp = jnp.where(lane == p, 1.0, jnp.where(lane == p + 1, 0.0, xp))
                xq = spread(ROWS + i // 2, i + 1)
                xq = jnp.where(lane == p + 1, 1.0, jnp.where(lane == p, 0.0, xq))
                xq = xq - ratio * xp
                xp_scaled = xp * ra
                xq_scaled = xq * (a * rdet)
                Z = jnp.where((row == i) & (lane == p), 1.0, X[k])
                if i + 2 < ROWS:
                    f0 = cols[i] * ra
                    f1 = (a * cols[i + 1] - b * cols[i]) * rdet
                    for q in rest:
                        cols[q] = cols[q] - f0 * firsts[q] - f1 * seconds[q]
                    m0 = jnp.where(row > i + 1, f0, 0.0)
                    m1 = jnp.where(row > i + 1, f1, 0.0)
                    Z = jnp.where((row > i + 1) & pair, 0.0, Z) - m0 * xp - m1 * xq
                X[k] = jnp.where(row == i + 1, xq, Z)
                if more:
                    g0, g1 = nexts[i], nexts[i + 1]
                    h0 = g0 * ra
                    g1 = a * g1 - b * g0
                    h1 = g1 * rdet
                    put(EXTRA + i, g0)
                    put(EXTRA + i + 1, g1 * ra)
                    for q in range(ROWS):
                        first, second = spread(EXTRA + i, q), spread(EXTRA + i + 1, q)
                        heads[t][q] = heads[t][q] - h0 * first - h1 * second
                    for q in rest:
                        nexts[q] = nexts[q] - h0 * firsts[q] - h1 * seconds[q]
                    X[k + 1] = jnp.where(pair, 0.0, X[k + 1]) - h0 * xp - h1 * xq
                for j in range(k + 2, reach):
                    g0 = spread_lane(X[j], p)
                    g1 = spread_lane(X[j], p + 1) - ratio * g0
                    X[j] = jnp.where(pair, 0.0, X[j]) - g0 * xp_scaled - g1 * xq_scaled
            s = lax.rsqrt(pivots)
            s = s * (1.5 - 0.5 * pivots * s * s)
            scaled = X[k] * s
            diagonal = jnp.where(lane == row + base, pivots * s, 0.0)
            out[0].append(jnp.where(lane > row + base, scaled, diagonal))
            out[1].append(jnp.where(lane <= row + base, scaled, 0.0))
            if k + 1 == stop and reach < count:
                begin = stop - group
                low, high = ROWS * begin, ROWS * stop
                uppers = jnp.concatenate(out[0][begin:stop], axis=0)
                lowers = jnp.concatenate(out[1][begin:stop], axis=0)
                after = lax.broadcasted_iota(jnp.int32, uppers.shape, 1) >= high
                change = exact_tn(uppers, jnp.where(after, uppers, lowers))
                here = (lane >= low) & (lane < high)
                for j in range(reach, count):
                    X[j] = jnp.where(here, 0.0, X[j]) - change[ROWS * j : ROWS * (j + 1)]
    return [(jnp.concatenate(u, axis=0), jnp.concatenate(v, axis=0)) for u, v in outs]


def factor(matrices, board):
    blocks = matrices[0].shape[0] // LANES
    if blocks == 1:
        return factor_small(matrices, board, GROUP)

    def cut(m, i, j):
        return m[LANES * i : LANES * (i + 1), LANES * j : LANES * (j + 1)]

    zero = jnp.zeros((LANES, LANES), jnp.float32)
    uppers = [{} for m in matrices]
    lowers = [{} for m in matrices]
    inverses = [{} for m in matrices]
    for j in range(blocks):
        heads = []
        for m, U, L in zip(matrices, uppers, lowers):
            head = cut(m, j, j)
            for k in range(j):
                head = head - exact_nt(L[j, k], L[j, k])
            heads.append(head)
        for m, U, L, V, (u, v) in zip(
            matrices, uppers, lowers, inverses, factor_small(heads, board, GROUP)
        ):
            U[j, j] = u
            V[j, j] = v
            for i in range(j + 1, blocks):
                right = cut(m, j, i)
                down = cut(m, i, j)
                for k in range(j):
                    right = right - exact_nn(L[j, k], U[k, i])
                    down = down - exact_nn(L[i, k], U[k, j])
                U[j, i] = exact_nn(v, right)
                L[i, j] = exact_nt(down, v)
    outs = []
    for U, L, V in zip(uppers, lowers, inverses):
        for i in range(blocks):
            for j in range(i):
                total = exact_nn(L[i, j], V[j, j])
                for k in range(j + 1, i):
                    total = total + exact_nn(L[i, k], V[k, j])
                V[i, j] = -exact_nn(V[i, i], total)
        whole = [
            jnp.concatenate(
                [
                    jnp.concatenate([D.get((i, j), zero) for j in range(blocks)], axis=1)
                    for i in range(blocks)
                ],
                axis=0,
            )
            for D in (U, V)
        ]
        outs.append(tuple(whole))
    return outs


def unit(side):
    row = lax.broadcasted_iota(jnp.int32, (side, side), 0)
    col = lax.broadcasted_iota(jnp.int32, (side, side), 1)
    return jnp.where(row == col, 1.0, 0.0)


def first_of(values):
    row = lax.broadcasted_iota(jnp.int32, (VECTOR, values.shape[1]), 0)
    return jnp.where(row == 0, values, 0.0)


def maps_kernel(transition_ref, sensing_ref, noise_ref, left_ref, right_ref, consts_ref):
    n = transition_ref.shape[0]
    transition = transition_ref[...]
    sensing = sensing_ref[...]
    noise = noise_ref[...]
    maps = jnp.concatenate([transition, dot_nn(sensing, transition)], axis=0)
    high, low, least = pieces(maps, 3)
    left_ref[...] = jnp.concatenate([high, low, least, high], axis=1)
    right_ref[...] = jnp.concatenate([high, high, low, least], axis=1)
    noise_sensed = dot_nt(noise, sensing)
    consts_ref[0:n, 0:n] = noise
    consts_ref[0:n, n:] = noise_sensed
    consts_ref[n:, 0:n] = jnp.zeros((sensing.shape[0], n), jnp.float32)
    consts_ref[n:, n:] = dot_nn(sensing, noise_sensed)


def window_kernel(
    steps,
    times,
    begin_ref,
    rows_ref,
    left_ref,
    right_ref,
    consts_ref,
    mean_ref,
    prior_ref,
    state_ref,
    info_ref,
    moved_ref,
    waiting_ref,
    inverse_ref,
    sensed_ref,
    board,
):
    n = prior_ref.shape[0]
    o = left_ref.shape[0] - n
    begin = begin_ref[0]
    eye_sense = unit(o)

    def wrap(t):
        return jnp.where(t >= times, t - times, t)

    def line_at(k):
        return rows_ref[pl.ds(wrap(begin + jnp.minimum(k, steps - 1)), 1), :]

    def first_spread(k, spread):
        line = line_at(k)
        return spread + consts_ref[n:, n:] + eye_sense * line[:, o:]

    moved_ref[0:n] = jnp.zeros((n, n), jnp.float32)
    moved_ref[n : 2 * n] = unit(n)
    moved_ref[2 * n :] = jnp.zeros((VECTOR, n), jnp.float32)
    waiting_ref[...] = jnp.zeros_like(waiting_ref)
    inverse_ref[...] = jnp.zeros_like(inverse_ref)
    info_ref[...] = jnp.zeros_like(info_ref)

    def through_sensed(spread):
        half = join_nt(left_moving(spread), right_ref[n:])
        return join_nn(left_ref[n:], right_moving(half))

    sensed_ref[...] = first_spread(
        0, jnp.where(begin == 0, through_sensed(prior_ref[...]), 0.0)
    )

    def update():
        white = join_nt(waiting_ref[...], inverse_ref[...])
        left = left_of(white)
        info_ref[...] = info_ref[...] + join_nt(left[n:], right_of(white[n : 2 * n]))
        return moved_ref[...] - join_nt(left, right_of(white[0:n]))

    def step(k, carry):
        ((_, inverse),) = factor_small([sensed_ref[...]], board)
        now = wrap(begin + k)
        later = wrap(now + 1)
        state = update()
        state = jnp.where(
            now == 0,
            jnp.concatenate(
                [prior_ref[...], jnp.zeros((n, n), jnp.float32), first_of(mean_ref[...])], axis=0
            ),
            state,
        )
        moved = join_nt(left_moving(state), right_ref[...])
        ahead = join_nn(left_ref[0:n], right_moving(moved[0:n])) + consts_ref[0:n]
        moved_ref[0:n] = ahead[:, 0:n]
        moved_ref[n:] = moved[n:, 0:n]
        waiting_ref[0:n] = left_of(ahead[:, n:])
        waiting_ref[n : 2 * n] = left_of(moved[n : 2 * n, n:])
        waiting_ref[2 * n :] = left_of(moved[2 * n :, n:] - first_of(line_at(k)[:, 0:o]))
        kept = through_sensed(jnp.where(later == 0, prior_ref[...], ahead[:, 0:n]))
        gained = exact_nt(join_nn(left_ref[n:], right_moving(ahead[:, n:])), inverse)
        gained = jnp.where(later == 0, 0.0, gained)
        sensed_ref[...] = first_spread(k + 1, kept - exact_nt(gained, gained))
        inverse_ref[...] = right_of(inverse)
        return carry

    lax.fori_loop(0, steps, step, 0)
    state = update()
    ((root, _),) = factor([state[0:n]], board)
    state_ref[0:n] = root
    state_ref[n:] = state[n:]


def meet_kernel(
    role_ref, state_ref, info_ref, far_state_ref, far_info_ref, packed_ref, board
):
    n = state_ref.shape[1]
    late = role_ref[0] == 1
    eye = unit(n)

    def of_cut(rows, near, far):
        return jnp.where(late, far[rows], near[rows])

    def of_middle(rows, near, far):
        return jnp.where(late, near[rows], far[rows])

    root_rows, move_rows, center_rows = slice(0, n), slice(n, 2 * n), slice(2 * n, 2 * n + VECTOR)
    info_rows, vector_rows = slice(0, n), slice(n, n + VECTOR)
    cut_root = of_cut(root_rows, state_ref, far_state_ref)
    cut_center = of_cut(center_rows, state_ref, far_state_ref)
    cut_info = of_cut(info_rows, info_ref, far_info_ref)
    cut_vector = of_cut(vector_rows, info_ref, far_info_ref)
    mid_root = of_middle(root_rows, state_ref, far_state_ref)
    move = of_middle(move_rows, state_ref, far_state_ref)
    mid_center = of_middle(center_rows, state_ref, far_state_ref)
    mid_info = of_middle(info_rows, info_ref, far_info_ref)
    mid_vector = of_middle(vector_rows, info_ref, far_info_ref)

    rooted = exact_nt(cut_info, mid_root)
    ((_, inner),) = factor([eye + exact_nn(mid_root, rooted)], board)
    carried = near_nn(inner, mid_root)
    mixing = near_nt(rooted, inner)
    kept = cut_info - near_nt(mixing, mixing)
    early_info = mid_info + near_nt(near_nn(move, kept), move)
    ((_, last),) = factor(
        [eye + exact_nn(cut_root, exact_nt(early_info, cut_root))], board
    )
    residue = -cut_vector - near_nn(mid_center, cut_info)
    residue_carried = near_nt(residue, carried)
    early_vector = near_nt(residue - near_nt(residue_carried, mixing), move) - mid_vector
    pull = early_vector - near_nn(cut_center, early_info)
    cut_root_t = cut_root.T
    through = move - near_nn(near_nn(move, mixing), carried)
    through_center = mid_center + near_nn(residue_carried, carried)
    carried_t = carried.T
    leftover = near_nt(carried_t, carried_t)
    late_root = near_nt(through.T, cut_root)
    early_root = near_nt(cut_root_t, last)
    early_center = cut_center + near_nt(near_nn(pull, early_root), early_root)
    root = near_nt(jnp.where(late, late_root, cut_root_t), last)
    cov = jnp.where(late, leftover, 0.0) + near_nt(root, root)
    late_center = near_nn(early_center, through) + through_center
    mean = jnp.where(late, late_center, early_center)[0:1]
    half = n // 2
    row, col = square(half)
    last_block = cov[half:, half:]
    diagonal = jnp.sum(jnp.where(row == col, last_block, 0.0), axis=0, keepdims=True)
    packed_ref[0:half, 0:half] = jnp.where(row >= col, cov[0:half, 0:half], last_block)
    packed_ref[0:half, half:] = cov[0:half, half:]
    line = lax.broadcasted_iota(jnp.int32, (ROWS, n), 0)
    diagonal = jnp.concatenate([diagonal, jnp.zeros_like(diagonal)], axis=1)
    packed_ref[half:] = jnp.where(line == 0, mean, jnp.where(line == 1, diagonal, 0.0))


def square(side):
    return (
        lax.broadcasted_iota(jnp.int32, (side, side), 0),
        lax.broadcasted_iota(jnp.int32, (side, side), 1),
    )


def unfold_kernel(packed_ref, mean_ref, cov_ref):
    half = packed_ref.shape[1] // 2
    row, col = square(half)
    both = packed_ref[0:half, 0:half]
    across = packed_ref[0:half, half:]
    above = jnp.where(row < col, both, 0.0)
    cov_ref[0, 0:half, 0:half] = jnp.where(row >= col, both, 0.0) + jnp.where(row > col, both, 0.0).T
    cov_ref[0, 0:half, half:] = across
    cov_ref[0, half:, 0:half] = across.T
    diagonal = jnp.where(row == col, packed_ref[half + 1 : half + 2, 0:half], 0.0)
    cov_ref[0, half:, half:] = above + above.T + diagonal
    mean_ref[...] = packed_ref[half : half + 1]


def begin_of(device, devices):
    quarter = devices // 4
    chip = device // 2
    upper = chip // quarter
    split = 2 * (chip - quarter * upper) + upper
    role = device % 2
    return (split + 1 + (1 - role) * (devices - devices // 2)) % devices


def gather_rows(rows, axis):
    devices = lax.axis_size(axis)
    return lax.all_to_all(
        jnp.broadcast_to(rows, (devices, rows.shape[1])), axis, 0, 0, tiled=True
    )


def shards(
    measurements, noise_levels, transition, sensing, process_noise, prior_mean, prior_covariance
):
    n = transition.shape[0]
    o = sensing.shape[0]
    devices = lax.axis_size("tm")
    half = devices // 2
    device = lax.axis_index("tm").astype(jnp.int32)
    role = device % 2
    begin = begin_of(device, devices)

    rows = gather_rows(jnp.concatenate([measurements, noise_levels], axis=1), "tm")
    vmem = pl.BlockSpec(memory_space=pltpu.VMEM)
    smem = pl.BlockSpec(memory_space=pltpu.SMEM)
    params = pltpu.CompilerParams(vmem_limit_bytes=48 * 1024 * 1024)

    def shape(*dims):
        return jax.ShapeDtypeStruct(dims, jnp.float32)

    passes = jax.ShapeDtypeStruct((n + o, 4 * n), jnp.bfloat16)
    left, right, consts = pl.pallas_call(
        maps_kernel,
        out_shape=(passes, passes, shape(n + o, n + o)),
        in_specs=[vmem] * 3,
        out_specs=(vmem, vmem, vmem),
        compiler_params=params,
    )(transition, sensing, process_noise)
    state, info = pl.pallas_call(
        functools.partial(window_kernel, half, devices),
        out_shape=(shape(2 * n + VECTOR, n), shape(n + VECTOR, n)),
        in_specs=[smem] + [vmem] * 6,
        out_specs=(vmem, vmem),
        scratch_shapes=[
            pltpu.VMEM((2 * n + VECTOR, n), jnp.float32),
            pltpu.VMEM((2 * n + VECTOR, 3 * o), jnp.bfloat16),
            pltpu.VMEM((o, 3 * o), jnp.bfloat16),
            pltpu.VMEM((o, o), jnp.float32),
            pltpu.VMEM((1, 2, BOARD, o), jnp.float32),
        ],
        compiler_params=params,
    )(begin.reshape(1), rows, left, right, consts, prior_mean.reshape(1, n), prior_covariance)
    swap = [(i, i ^ 1) for i in range(devices)]
    far_state = lax.ppermute(state, "tm", swap)
    far_info = lax.ppermute(info, "tm", swap)
    packed = pl.pallas_call(
        meet_kernel,
        out_shape=shape(n // 2 + ROWS, n),
        in_specs=[smem] + [vmem] * 4,
        out_specs=vmem,
        scratch_shapes=[pltpu.VMEM((1, 2, BOARD, LANES), jnp.float32)],
        compiler_params=params,
    )(role.reshape(1), state, info, far_state, far_info)
    home = []
    for i in range(devices):
        above = i >= half
        spot = 2 * ((i - half if above else i) // 2) + (1 if above else 0)
        home.append((i, spot + half if i % 2 else spot))
    return pl.pallas_call(
        unfold_kernel,
        out_shape=(shape(1, n), shape(1, n, n)),
        in_specs=[vmem],
        out_specs=(vmem, vmem),
        compiler_params=params,
    )(lax.ppermute(packed, "tm", home))


def solution(mesh):
    return jax.shard_map(
        shards,
        mesh=mesh,
        in_specs=(P("tm", None), P("tm", None), P(), P(), P(), P(), P()),
        out_specs=(P("tm", None), P("tm", None, None)),
        check_vma=False,
    )
```

```python
import functools

import jax
import jax.numpy as jnp
from jax import lax
from jax.experimental import pallas as pl
from jax.experimental.pallas import tpu as pltpu
from jax.sharding import PartitionSpec as P

ROWS = 8
LANES = 128
VECTOR = 16
GROUP = 4
LEAD = 2
EXTRA = ROWS + ROWS // 2
BOARD = ROWS * (EXTRA + ROWS)


def dot_nn(left, right):
    return lax.dot_general(
        left,
        right,
        (((1,), (0,)), ((), ())),
        precision=lax.Precision.HIGHEST,
        preferred_element_type=jnp.float32,
    )


def dot_nt(left, right):
    return lax.dot_general(
        left,
        right,
        (((1,), (1,)), ((), ())),
        precision=lax.Precision.HIGHEST,
        preferred_element_type=jnp.float32,
    )


def pieces(x, count):
    out = []
    for _ in range(count):
        out.append(x.astype(jnp.bfloat16))
        x = x - out[-1].astype(jnp.float32)
    return out


def left_of(x):
    high, low = pieces(x, 2)
    return jnp.concatenate([high, low, high], axis=1)


def right_of(x):
    high, low = pieces(x, 2)
    return jnp.concatenate([high, high, low], axis=1)


def left_moving(x):
    high, low = pieces(x, 2)
    return jnp.concatenate([high, low, high, high], axis=1)


def right_moving(x):
    high, low = pieces(x, 2)
    return jnp.concatenate([high, high, high, low], axis=0)


def join_nn(left, right):
    return lax.dot_general(
        left, right, (((1,), (0,)), ((), ())), preferred_element_type=jnp.float32
    )


def join_nt(left, right):
    return lax.dot_general(
        left, right, (((1,), (1,)), ((), ())), preferred_element_type=jnp.float32
    )


def spread_lane(x, lane):
    return jnp.broadcast_to(x[:, lane : lane + 1], x.shape)


def exact_tn(left, right):
    a, b, c = pieces(left, 3)
    p, q, r = pieces(right, 3)
    return lax.dot_general(
        jnp.concatenate([a, a, b, a, b, c], axis=0),
        jnp.concatenate([p, q, p, r, q, p], axis=0),
        (((0,), (0,)), ((), ())),
        preferred_element_type=jnp.float32,
    )


def exact_nt(left, right):
    a, b, c = pieces(left, 3)
    p, q, r = pieces(right, 3)
    return join_nt(
        jnp.concatenate([a, a, b, a, b, c], axis=1), jnp.concatenate([p, q, p, r, q, p], axis=1)
    )


def exact_nn(left, right):
    a, b, c = pieces(left, 3)
    p, q, r = pieces(right, 3)
    return join_nn(
        jnp.concatenate([a, a, b, a, b, c], axis=1), jnp.concatenate([p, q, p, r, q, p], axis=0)
    )


def near_nn(left, right):
    high, low = pieces(right, 2)
    return join_nn(left_of(left), jnp.concatenate([high, high, low], axis=0))


def near_nt(left, right):
    return join_nt(left_of(left), right_of(right))


def factor_small(matrices, board, group=None):
    side = matrices[0].shape[0]
    count = side // ROWS
    group = group or count
    shape = (ROWS, side)
    row = lax.broadcasted_iota(jnp.int32, shape, 0)
    lane = lax.broadcasted_iota(jnp.int32, shape, 1)
    tasks = [[m[ROWS * k : ROWS * (k + 1)] for k in range(count)] for m in matrices]
    outs = [([], []) for m in matrices]
    heads = [[spread_lane(X[0], i) for i in range(ROWS)] for X in tasks]
    for k in range(count):
        base = ROWS * k
        more = k + 1 < count
        stop = min(count, (k // group + 1) * group)
        reach = min(count, stop + LEAD)
        for t, (X, out) in enumerate(zip(tasks, outs)):

            def put(slot, values):
                board[t, k % 2, ROWS * slot : ROWS * (slot + 1)] = values

            def spread(slot, r):
                at = ROWS * slot + r
                return jnp.broadcast_to(board[t, k % 2, at : at + 1], shape)

            cols = heads[t]
            for i in range(ROWS):
                put(i, cols[i])
            block = {(r, i): spread(i, r) for i in range(ROWS) for r in range(i, ROWS)}
            nexts = [spread_lane(X[k + 1], base + i) for i in range(ROWS)] if more else []
            heads[t] = [spread_lane(X[k + 1], base + ROWS + i) for i in range(ROWS)] if more else []
            pivots = jnp.ones(shape, jnp.float32)
            for i in range(0, ROWS, 2):
                p = base + i
                pair = (lane == p) | (lane == p + 1)
                a, b, c = block[i, i], block[i + 1, i], block[i + 1, i + 1]
                det = a * c - b * b
                ra = pltpu.reciprocal(a, approx=True)
                rdet = pltpu.reciprocal(det, approx=True)
                ratio = b * ra
                rest = range(i + 2, ROWS)
                firsts = {q: block[q, i] for q in rest}
                mixed = {q: a * block[q, i + 1] - b * firsts[q] for q in rest}
                seconds = {q: mixed[q] * ra for q in rest}
                for q in rest:
                    for r in range(q, ROWS):
                        block[r, q] = (
                            block[r, q] - (firsts[r] * ra) * firsts[q] - (mixed[r] * rdet) * seconds[q]
                        )
                pivots = jnp.where(row == i, a, pivots)
                pivots = jnp.where(row == i + 1, det * ra, pivots)
                put(ROWS + i // 2, X[k])
                xp = spread(ROWS + i // 2, i)
                xp = jnp.where(lane == p, 1.0, jnp.where(lane == p + 1, 0.0, xp))
                xq = spread(ROWS + i // 2, i + 1)
                xq = jnp.where(lane == p + 1, 1.0, jnp.where(lane == p, 0.0, xq))
                xq = xq - ratio * xp
                xp_scaled = xp * ra
                xq_scaled = xq * (a * rdet)
                Z = jnp.where((row == i) & (lane == p), 1.0, X[k])
                if i + 2 < ROWS:
                    f0 = cols[i] * ra
                    f1 = (a * cols[i + 1] - b * cols[i]) * rdet
                    for q in rest:
                        cols[q] = cols[q] - f0 * firsts[q] - f1 * seconds[q]
                    m0 = jnp.where(row > i + 1, f0, 0.0)
                    m1 = jnp.where(row > i + 1, f1, 0.0)
                    Z = jnp.where((row > i + 1) & pair, 0.0, Z) - m0 * xp - m1 * xq
                X[k] = jnp.where(row == i + 1, xq, Z)
                if more:
                    g0, g1 = nexts[i], nexts[i + 1]
                    h0 = g0 * ra
                    g1 = a * g1 - b * g0
                    h1 = g1 * rdet
                    put(EXTRA + i, g0)
                    put(EXTRA + i + 1, g1 * ra)
                    for q in range(ROWS):
                        first, second = spread(EXTRA + i, q), spread(EXTRA + i + 1, q)
                        heads[t][q] = heads[t][q] - h0 * first - h1 * second
                    for q in rest:
                        nexts[q] = nexts[q] - h0 * firsts[q] - h1 * seconds[q]
                    X[k + 1] = jnp.where(pair, 0.0, X[k + 1]) - h0 * xp - h1 * xq
                for j in range(k + 2, reach):
                    g0 = spread_lane(X[j], p)
                    g1 = spread_lane(X[j], p + 1) - ratio * g0
                    X[j] = jnp.where(pair, 0.0, X[j]) - g0 * xp_scaled - g1 * xq_scaled
            s = lax.rsqrt(pivots)
            s = s * (1.5 - 0.5 * pivots * s * s)
            scaled = X[k] * s
            diagonal = jnp.where(lane == row + base, pivots * s, 0.0)
            out[0].append(jnp.where(lane > row + base, scaled, diagonal))
            out[1].append(jnp.where(lane <= row + base, scaled, 0.0))
            if k + 1 == stop and reach < count:
                begin = stop - group
                low, high = ROWS * begin, ROWS * stop
                uppers = jnp.concatenate(out[0][begin:stop], axis=0)
                lowers = jnp.concatenate(out[1][begin:stop], axis=0)
                after = lax.broadcasted_iota(jnp.int32, uppers.shape, 1) >= high
                change = exact_tn(uppers, jnp.where(after, uppers, lowers))
                here = (lane >= low) & (lane < high)
                for j in range(reach, count):
                    X[j] = jnp.where(here, 0.0, X[j]) - change[ROWS * j : ROWS * (j + 1)]
    return [(jnp.concatenate(u, axis=0), jnp.concatenate(v, axis=0)) for u, v in outs]


def factor(matrices, board):
    blocks = matrices[0].shape[0] // LANES
    if blocks == 1:
        return factor_small(matrices, board, GROUP)

    def cut(m, i, j):
        return m[LANES * i : LANES * (i + 1), LANES * j : LANES * (j + 1)]

    zero = jnp.zeros((LANES, LANES), jnp.float32)
    uppers = [{} for m in matrices]
    lowers = [{} for m in matrices]
    inverses = [{} for m in matrices]
    for j in range(blocks):
        heads = []
        for m, U, L in zip(matrices, uppers, lowers):
            head = cut(m, j, j)
            for k in range(j):
                head = head - exact_nt(L[j, k], L[j, k])
            heads.append(head)
        for m, U, L, V, (u, v) in zip(
            matrices, uppers, lowers, inverses, factor_small(heads, board, GROUP)
        ):
            U[j, j] = u
            V[j, j] = v
            for i in range(j + 1, blocks):
                right = cut(m, j, i)
                down = cut(m, i, j)
                for k in range(j):
                    right = right - exact_nn(L[j, k], U[k, i])
                    down = down - exact_nn(L[i, k], U[k, j])
                U[j, i] = exact_nn(v, right)
                L[i, j] = exact_nt(down, v)
    outs = []
    for U, L, V in zip(uppers, lowers, inverses):
        for i in range(blocks):
            for j in range(i):
                total = exact_nn(L[i, j], V[j, j])
                for k in range(j + 1, i):
                    total = total + exact_nn(L[i, k], V[k, j])
                V[i, j] = -exact_nn(V[i, i], total)
        whole = [
            jnp.concatenate(
                [
                    jnp.concatenate([D.get((i, j), zero) for j in range(blocks)], axis=1)
                    for i in range(blocks)
                ],
                axis=0,
            )
            for D in (U, V)
        ]
        outs.append(tuple(whole))
    return outs


def unit(side):
    row = lax.broadcasted_iota(jnp.int32, (side, side), 0)
    col = lax.broadcasted_iota(jnp.int32, (side, side), 1)
    return jnp.where(row == col, 1.0, 0.0)


def first_of(values):
    row = lax.broadcasted_iota(jnp.int32, (VECTOR, values.shape[1]), 0)
    return jnp.where(row == 0, values, 0.0)


def maps_kernel(transition_ref, sensing_ref, noise_ref, left_ref, right_ref, consts_ref):
    n = transition_ref.shape[0]
    transition = transition_ref[...]
    sensing = sensing_ref[...]
    noise = noise_ref[...]
    maps = jnp.concatenate([transition, dot_nn(sensing, transition)], axis=0)
    high, low, least = pieces(maps, 3)
    left_ref[...] = jnp.concatenate([high, low, least, high], axis=1)
    right_ref[...] = jnp.concatenate([high, high, low, least], axis=1)
    noise_sensed = dot_nt(noise, sensing)
    consts_ref[0:n, 0:n] = noise
    consts_ref[0:n, n:] = noise_sensed
    consts_ref[n:, 0:n] = jnp.zeros((sensing.shape[0], n), jnp.float32)
    consts_ref[n:, n:] = dot_nn(sensing, noise_sensed)


def window_kernel(
    steps,
    times,
    begin_ref,
    rows_ref,
    left_ref,
    right_ref,
    consts_ref,
    mean_ref,
    prior_ref,
    state_ref,
    info_ref,
    moved_ref,
    waiting_ref,
    inverse_ref,
    sensed_ref,
    board,
):
    n = prior_ref.shape[0]
    o = left_ref.shape[0] - n
    begin = begin_ref[0]
    eye_sense = unit(o)

    def wrap(t):
        return jnp.where(t >= times, t - times, t)

    def line_at(k):
        return rows_ref[pl.ds(wrap(begin + jnp.minimum(k, steps - 1)), 1), :]

    def first_spread(k, spread):
        line = line_at(k)
        return spread + consts_ref[n:, n:] + eye_sense * line[:, o:]

    moved_ref[0:n] = jnp.zeros((n, n), jnp.float32)
    moved_ref[n : 2 * n] = unit(n)
    moved_ref[2 * n :] = jnp.zeros((VECTOR, n), jnp.float32)
    waiting_ref[...] = jnp.zeros_like(waiting_ref)
    inverse_ref[...] = jnp.zeros_like(inverse_ref)
    info_ref[...] = jnp.zeros_like(info_ref)

    def through_sensed(spread):
        half = join_nt(left_moving(spread), right_ref[n:])
        return join_nn(left_ref[n:], right_moving(half))

    sensed_ref[...] = first_spread(
        0, jnp.where(begin == 0, through_sensed(prior_ref[...]), 0.0)
    )

    def update():
        white = join_nt(waiting_ref[...], inverse_ref[...])
        left = left_of(white)
        info_ref[...] = info_ref[...] + join_nt(left[n:], right_of(white[n : 2 * n]))
        return moved_ref[...] - join_nt(left, right_of(white[0:n]))

    def step(k, carry):
        ((_, inverse),) = factor_small([sensed_ref[...]], board)
        now = wrap(begin + k)
        later = wrap(now + 1)
        state = update()
        state = jnp.where(
            now == 0,
            jnp.concatenate(
                [prior_ref[...], jnp.zeros((n, n), jnp.float32), first_of(mean_ref[...])], axis=0
            ),
            state,
        )
        moved = join_nt(left_moving(state), right_ref[...])
        ahead = join_nn(left_ref[0:n], right_moving(moved[0:n])) + consts_ref[0:n]
        moved_ref[0:n] = ahead[:, 0:n]
        moved_ref[n:] = moved[n:, 0:n]
        waiting_ref[0:n] = left_of(ahead[:, n:])
        waiting_ref[n : 2 * n] = left_of(moved[n : 2 * n, n:])
        waiting_ref[2 * n :] = left_of(moved[2 * n :, n:] - first_of(line_at(k)[:, 0:o]))
        kept = through_sensed(jnp.where(later == 0, prior_ref[...], ahead[:, 0:n]))
        gained = exact_nt(join_nn(left_ref[n:], right_moving(ahead[:, n:])), inverse)
        gained = jnp.where(later == 0, 0.0, gained)
        sensed_ref[...] = first_spread(k + 1, kept - exact_nt(gained, gained))
        inverse_ref[...] = right_of(inverse)
        return carry

    lax.fori_loop(0, steps, step, 0)
    state = update()
    ((root, _),) = factor([state[0:n]], board)
    state_ref[0:n] = root
    state_ref[n:] = state[n:]


def meet_kernel(
    role_ref, state_ref, info_ref, far_state_ref, far_info_ref, packed_ref, board
):
    n = state_ref.shape[1]
    late = role_ref[0] == 1
    eye = unit(n)

    def of_cut(rows, near, far):
        return jnp.where(late, far[rows], near[rows])

    def of_middle(rows, near, far):
        return jnp.where(late, near[rows], far[rows])

    root_rows, move_rows, center_rows = slice(0, n), slice(n, 2 * n), slice(2 * n, 2 * n + VECTOR)
    info_rows, vector_rows = slice(0, n), slice(n, n + VECTOR)
    cut_root = of_cut(root_rows, state_ref, far_state_ref)
    cut_center = of_cut(center_rows, state_ref, far_state_ref)
    cut_info = of_cut(info_rows, info_ref, far_info_ref)
    cut_vector = of_cut(vector_rows, info_ref, far_info_ref)
    mid_root = of_middle(root_rows, state_ref, far_state_ref)
    move = of_middle(move_rows, state_ref, far_state_ref)
    mid_center = of_middle(center_rows, state_ref, far_state_ref)
    mid_info = of_middle(info_rows, info_ref, far_info_ref)
    mid_vector = of_middle(vector_rows, info_ref, far_info_ref)

    rooted = exact_nt(cut_info, mid_root)
    ((_, inner),) = factor([eye + exact_nn(mid_root, rooted)], board)
    carried = near_nn(inner, mid_root)
    mixing = near_nt(rooted, inner)
    kept = cut_info - near_nt(mixing, mixing)
    early_info = mid_info + near_nt(near_nn(move, kept), move)
    ((_, last),) = factor(
        [eye + exact_nn(cut_root, exact_nt(early_info, cut_root))], board
    )
    residue = -cut_vector - near_nn(mid_center, cut_info)
    residue_carried = near_nt(residue, carried)
    early_vector = near_nt(residue - near_nt(residue_carried, mixing), move) - mid_vector
    pull = early_vector - near_nn(cut_center, early_info)
    cut_root_t = cut_root.T
    through = move - near_nn(near_nn(move, mixing), carried)
    through_center = mid_center + near_nn(residue_carried, carried)
    carried_t = carried.T
    leftover = near_nt(carried_t, carried_t)
    late_root = near_nt(through.T, cut_root)
    early_root = near_nt(cut_root_t, last)
    early_center = cut_center + near_nt(near_nn(pull, early_root), early_root)
    root = near_nt(jnp.where(late, late_root, cut_root_t), last)
    cov = jnp.where(late, leftover, 0.0) + near_nt(root, root)
    late_center = near_nn(early_center, through) + through_center
    mean = jnp.where(late, late_center, early_center)[0:1]
    half = n // 2
    row, col = square(half)
    last_block = cov[half:, half:]
    diagonal = jnp.sum(jnp.where(row == col, last_block, 0.0), axis=0, keepdims=True)
    packed_ref[0:half, 0:half] = jnp.where(row >= col, cov[0:half, 0:half], last_block)
    packed_ref[0:half, half:] = cov[0:half, half:]
    line = lax.broadcasted_iota(jnp.int32, (ROWS, n), 0)
    diagonal = jnp.concatenate([diagonal, jnp.zeros_like(diagonal)], axis=1)
    packed_ref[half:] = jnp.where(line == 0, mean, jnp.where(line == 1, diagonal, 0.0))


def square(side):
    return (
        lax.broadcasted_iota(jnp.int32, (side, side), 0),
        lax.broadcasted_iota(jnp.int32, (side, side), 1),
    )


def unfold_kernel(packed_ref, mean_ref, cov_ref):
    half = packed_ref.shape[1] // 2
    row, col = square(half)
    both = packed_ref[0:half, 0:half]
    across = packed_ref[0:half, half:]
    above = jnp.where(row < col, both, 0.0)
    cov_ref[0, 0:half, 0:half] = jnp.where(row >= col, both, 0.0) + jnp.where(row > col, both, 0.0).T
    cov_ref[0, 0:half, half:] = across
    cov_ref[0, half:, 0:half] = across.T
    diagonal = jnp.where(row == col, packed_ref[half + 1 : half + 2, 0:half], 0.0)
    cov_ref[0, half:, half:] = above + above.T + diagonal
    mean_ref[...] = packed_ref[half : half + 1]


def begin_of(device, devices):
    quarter = devices // 4
    chip = device // 2
    upper = chip // quarter
    split = 2 * (chip - quarter * upper) + upper
    role = device % 2
    return (split + 1 + (1 - role) * (devices - devices // 2)) % devices


def gather_rows(parts, axis):
    devices = lax.axis_size(axis)
    copies = [jnp.broadcast_to(part, (devices, part.shape[1])) for part in parts]
    return lax.all_to_all(jnp.concatenate(copies, axis=1), axis, 0, 0, tiled=True)


def shards(
    measurements, noise_levels, transition, sensing, process_noise, prior_mean, prior_covariance
):
    n = transition.shape[0]
    o = sensing.shape[0]
    devices = lax.axis_size("tm")
    half = devices // 2
    device = lax.axis_index("tm").astype(jnp.int32)
    role = device % 2
    begin = begin_of(device, devices)

    rows = gather_rows([measurements, noise_levels], "tm")
    vmem = pl.BlockSpec(memory_space=pltpu.VMEM)
    smem = pl.BlockSpec(memory_space=pltpu.SMEM)
    params = pltpu.CompilerParams(vmem_limit_bytes=48 * 1024 * 1024)

    def shape(*dims):
        return jax.ShapeDtypeStruct(dims, jnp.float32)

    passes = jax.ShapeDtypeStruct((n + o, 4 * n), jnp.bfloat16)
    left, right, consts = pl.pallas_call(
        maps_kernel,
        out_shape=(passes, passes, shape(n + o, n + o)),
        in_specs=[vmem] * 3,
        out_specs=(vmem, vmem, vmem),
        compiler_params=params,
    )(transition, sensing, process_noise)
    state, info = pl.pallas_call(
        functools.partial(window_kernel, half, devices),
        out_shape=(shape(2 * n + VECTOR, n), shape(n + VECTOR, n)),
        in_specs=[smem] + [vmem] * 6,
        out_specs=(vmem, vmem),
        scratch_shapes=[
            pltpu.VMEM((2 * n + VECTOR, n), jnp.float32),
            pltpu.VMEM((2 * n + VECTOR, 3 * o), jnp.bfloat16),
            pltpu.VMEM((o, 3 * o), jnp.bfloat16),
            pltpu.VMEM((o, o), jnp.float32),
            pltpu.VMEM((1, 2, BOARD, o), jnp.float32),
        ],
        compiler_params=params,
    )(begin.reshape(1), rows, left, right, consts, prior_mean.reshape(1, n), prior_covariance)
    swap = [(i, i ^ 1) for i in range(devices)]
    far_state = lax.ppermute(state, "tm", swap)
    far_info = lax.ppermute(info, "tm", swap)
    packed = pl.pallas_call(
        meet_kernel,
        out_shape=shape(n // 2 + ROWS, n),
        in_specs=[smem] + [vmem] * 4,
        out_specs=vmem,
        scratch_shapes=[pltpu.VMEM((1, 2, BOARD, LANES), jnp.float32)],
        compiler_params=params,
    )(role.reshape(1), state, info, far_state, far_info)
    home = []
    for i in range(devices):
        above = i >= half
        spot = 2 * ((i - half if above else i) // 2) + (1 if above else 0)
        home.append((i, spot + half if i % 2 else spot))
    return pl.pallas_call(
        unfold_kernel,
        out_shape=(shape(1, n), shape(1, n, n)),
        in_specs=[vmem],
        out_specs=(vmem, vmem),
        compiler_params=params,
    )(lax.ppermute(packed, "tm", home))


def solution(mesh):
    return jax.shard_map(
        shards,
        mesh=mesh,
        in_specs=(P("tm", None), P("tm", None), P(), P(), P(), P(), P()),
        out_specs=(P("tm", None), P("tm", None, None)),
        check_vma=False,
    )
```
